512 devices in a mesh: seqhi: 32 (over z, core), seqlo: 16 (over x, y).
Axes of the slice: x: 4, y: 4, z: 16, core: 2. Of those that a mesh axis runs over, the one named last changes fastest.
Arguments:
- queries: bfloat16 [65536, 1024], P(('seqhi', 'seqlo')), may hold values from -8 to 8
- key_rows: bfloat16 [65536, 1024], P(('seqhi', 'seqlo')), may hold values from -8 to 8
- value_rows: bfloat16 [65536, 1024], P(('seqhi', 'seqlo')), may hold values from -10 to 10
Outputs:
- attended: bfloat16 [65536, 1024], P(('seqhi', 'seqlo'))
The draws below stay inside these ranges and needn't reach their ends.
All inputs are finite; a program needn't handle non-finite values.
Results may differ from the reference program's by a relative error of at most 0.012.
Values may be sent and summed in bfloat16 or wider, within the bound.
No kernel may reach another device: no remote copies, remote signals or barrier semaphores. Data moves between devices by JAX's collectives and lax.ppermute only.
A program may use at most 64 MiB of HBM per device.

```python
import math
import jax
import jax.numpy as jnp
from jax import lax

HEADS = 16
HEAD = 64
BLOCK = 128
TOKENS = 65536


def layered(key):
    width = HEADS * HEAD
    scale_count = TOKENS.bit_length()
    each = 1.5 / math.sqrt(scale_count)
    total = jnp.zeros((TOKENS, width), jnp.float32)
    for level in range(scale_count):
        stride = 2 ** level
        region_count = (TOKENS + stride - 1) // stride
        table = jax.random.normal(jax.random.fold_in(key, 100 + level), (region_count, width), jnp.float32)
        widened = jnp.broadcast_to(table[:, None, :], (region_count, stride, width)).reshape(region_count * stride, width)
        total = total + each * widened[:TOKENS]
    return total


def stepped(key, finest, amounts):
    width = HEADS * HEAD
    total = jnp.zeros((TOKENS, width), jnp.float32)
    for level in range(len(amounts)):
        stride = finest * 2 ** level
        region_count = (TOKENS + stride - 1) // stride
        table = jax.random.normal(jax.random.fold_in(key, 200 + level), (region_count, width), jnp.float32)
        widened = jnp.broadcast_to(table[:, None, :], (region_count, stride, width)).reshape(region_count * stride, width)
        total = total + amounts[level] * widened[:TOKENS]
    return total


def draw_queries(key, part):
    own_key = jax.random.fold_in(key, 11)
    key_rough, key_layer = jax.random.split(own_key)
    shared = layered(key_layer)
    rough = 1.6 * jax.random.normal(key_rough, (TOKENS, HEADS * HEAD), jnp.float32)
    base = jnp.clip(shared + rough, -8.0, 8.0)
    return base.astype(jnp.bfloat16)


def draw_key_rows(key, part):
    own_key = jax.random.fold_in(key, 12)
    key_rough, key_layer = jax.random.split(own_key)
    shared = layered(key_layer)
    rough = 1.6 * jax.random.normal(key_rough, (TOKENS, HEADS * HEAD), jnp.float32)
    base = jnp.clip(shared + rough, -8.0, 8.0)
    return base.astype(jnp.bfloat16)


def draw_value_rows(key, part):
    own_key = jax.random.fold_in(key, 13)
    key_rough, key_table, key_steps = jax.random.split(own_key, 3)
    region = jnp.arange(TOKENS, dtype=jnp.int32) * 64 // TOKENS
    table = jnp.clip(0.8 * jax.random.normal(key_table, (64, HEADS * HEAD), jnp.float32), -4.0, 4.0)
    offset = table[region] + stepped(key_steps, max(BLOCK // 8, 1), (0.6, 0.6, 0.6, 2.0, 2.0, 2.0))
    rough = jnp.clip(jax.random.normal(key_rough, (TOKENS, HEADS * HEAD), jnp.float32), -4.0, 4.0)
    return jnp.clip(offset + rough, -10.0, 10.0).astype(jnp.bfloat16)


def setup_inputs(seed: int = 0) -> dict:
    arg_keys = jax.random.split(jax.random.key(seed), 4)
    return {
        "queries": draw_queries(jax.random.fold_in(arg_keys[3], 71), 0),
        "key_rows": draw_key_rows(jax.random.fold_in(arg_keys[3], 71), 0),
        "value_rows": draw_value_rows(jax.random.fold_in(arg_keys[3], 71), 0),
    }


floor_score = -1e+30

def coarsen(member):
    paired = member.reshape(member.shape[0] // 2, 2, member.shape[1]).astype(jnp.float32)
    return (0.5 * (paired[:, 0] + paired[:, 1])).astype(jnp.bfloat16)

def admit(row_ids, col_ids, height, row_count):
    allowed = (col_ids >= 0) & (col_ids < row_count) & (jnp.abs(row_ids // BLOCK - col_ids // BLOCK) <= 1)
    if height > 0:
        allowed = allowed & (jnp.abs(2 * row_ids // BLOCK - 2 * col_ids // BLOCK) > 1)
    return allowed

def attend(level_rows, key_block, value_block, allowed, weight):
    row_count = level_rows.shape[0]
    col_count = key_block.shape[0]
    q_heads = level_rows.astype(jnp.float32).reshape(row_count, HEADS, HEAD)
    k_heads = key_block.astype(jnp.float32).reshape(col_count, HEADS, HEAD)
    v_heads = value_block.astype(jnp.float32).reshape(col_count, HEADS, HEAD)
    scores = jnp.einsum('qhd,khd->hqk', q_heads, k_heads) * (1.0 / math.sqrt(HEAD))
    scores = jnp.where(allowed[None], scores, floor_score)
    maxima = lax.optimization_barrier(jnp.max(scores, axis=2))
    exp_terms = jnp.where(allowed[None], jnp.exp(scores - maxima[:, :, None]), 0.0)
    totals = weight * lax.optimization_barrier(jnp.sum(exp_terms, axis=2))
    low_terms = lax.optimization_barrier(exp_terms.astype(jnp.bfloat16)).astype(jnp.float32)
    weighted = weight * jnp.einsum('hqk,khd->qhd', low_terms, v_heads)
    return (maxima.T, totals.T, weighted)

def combine(left_terms, right_terms):
    maxima = jnp.maximum(left_terms[0], right_terms[0])
    scale_one = jnp.exp(left_terms[0] - maxima)
    scale_two = jnp.exp(right_terms[0] - maxima)
    return (maxima, left_terms[1] * scale_one + right_terms[1] * scale_two, left_terms[2] * scale_one[:, :, None] + right_terms[2] * scale_two[:, :, None])

def level_terms(level_queries, level_keys, level_values, height):
    row_count = level_queries.shape[0]
    block_count = row_count // BLOCK
    padding = jnp.zeros((BLOCK, level_keys.shape[1]), jnp.bfloat16)
    keys_padded = jnp.concatenate([padding, level_keys, padding], 0)
    values_padded = jnp.concatenate([padding, level_values, padding], 0)

    def one_block(block_index):
        anchor = block_index * BLOCK
        query_block = lax.dynamic_slice_in_dim(level_queries, anchor, BLOCK, 0)
        key_block = lax.dynamic_slice_in_dim(keys_padded, anchor, 3 * BLOCK, 0)
        value_block = lax.dynamic_slice_in_dim(values_padded, anchor, 3 * BLOCK, 0)
        row_ids = anchor + jnp.arange(BLOCK, dtype=jnp.int32)
        col_ids = anchor - BLOCK + jnp.arange(3 * BLOCK, dtype=jnp.int32)
        allowed = admit(row_ids[:, None], col_ids[None, :], height, row_count)
        return attend(query_block, key_block, value_block, allowed, 2.0 ** height)
    maxima, totals, weighted = lax.map(one_block, jnp.arange(block_count, dtype=jnp.int32))
    return (maxima.reshape(row_count, HEADS), totals.reshape(row_count, HEADS), weighted.reshape(row_count, HEADS, HEAD))

def reference(queries, key_rows, value_rows):
    height_count = (TOKENS // BLOCK).bit_length() - 1
    level_queries, level_keys, level_values = (queries, key_rows, value_rows)
    per_height = []
    for height in range(height_count):
        per_height.append(level_terms(level_queries, level_keys, level_values, height))
        level_queries = coarsen(level_queries)
        level_keys = coarsen(level_keys)
        level_values = coarsen(level_values)
    merged = per_height[-1]
    for height in range(height_count - 2, -1, -1):
        merged = combine(tuple((jnp.repeat(member, 2, axis=0) for member in merged)), per_height[height])
    maxima, totals, weighted = merged
    return (weighted / totals[:, :, None]).reshape(TOKENS, HEADS * HEAD).astype(jnp.bfloat16)
```

```python
import math

import jax
import jax.numpy as jnp
from jax import lax
from jax.experimental import pallas as pl
from jax.experimental.pallas import tpu as pltpu
from jax.sharding import PartitionSpec as P

HEADS = 16
HEAD = 64
BLOCK = 128
NEVER = -1e30
SCALE = math.log2(math.e) / math.sqrt(HEAD)
TILES = 16
OFFSET = {1: 0, 2: 8, 3: 12, 4: 14}
COUNT = {0: 16, 1: 8, 2: 4, 3: 2, 4: 1}
ROWS = 72
PACKED = {5: 0, 6: 64, 7: 96, 8: 112}

VMEM = pl.BlockSpec(memory_space=pltpu.VMEM)
SMEM = pl.BlockSpec(memory_space=pltpu.SMEM)
PARAMS = pltpu.CompilerParams(vmem_limit_bytes=48 * 1024 * 1024)


def iota(shape, dim):
    return lax.broadcasted_iota(jnp.int32, shape, dim)


def mm(a, b):
    return jnp.dot(a, b, preferred_element_type=jnp.float32)


def split_kernel(q_ref, k_ref, v_ref, out_ref):
    for pair in range(HEADS // 2):
        for place, ref in enumerate((q_ref, k_ref, v_ref)):
            turned = ref[:, 128 * pair : 128 * pair + 128].T
            out_ref[2 * pair, 64 * place : 64 * place + 64, :] = turned[:64]
            out_ref[2 * pair + 1, 64 * place : 64 * place + 64, :] = turned[64:]


def join_kernel(in_ref, out_ref):
    for pair in range(HEADS // 2):
        both = jnp.concatenate([in_ref[2 * pair], in_ref[2 * pair + 1]], axis=0)
        out_ref[:, 128 * pair : 128 * pair + 128] = both.T


def coarse_kernel(plane_ref, x_ref, tiles_ref, queries_ref, left_ref, right_ref, far_ref):
    plane = plane_ref[0]
    halve = jnp.where(iota((256, 128), 0) // 2 == iota((256, 128), 1), 0.5, 0.0).astype(jnp.bfloat16)
    finer = [x_ref[i] for i in range(TILES)]
    for level in range(1, 5):
        coarser = []
        for i in range(COUNT[level]):
            pair = jnp.concatenate([finer[2 * i], finer[2 * i + 1]], axis=1)
            tile = mm(pair, halve).astype(jnp.bfloat16)
            tiles_ref[OFFSET[level] + i] = tile
            coarser.append(tile)
        left_ref[level] = coarser[0][64:]
        right_ref[level] = coarser[-1][64:]
        finer = coarser
    left_ref[0] = x_ref[0, 64:]
    right_ref[0] = x_ref[TILES - 1, 64:]
    tile = finer[0]
    small = []
    for level in range(5, 9):
        tile = mm(tile, halve[:128]).astype(jnp.bfloat16)
        small.append(tile)
    lanes = iota((64, 128), 1)
    packed = small[0][:64].astype(jnp.float32)
    for level in range(6, 9):
        moved = pltpu.roll(small[level - 5][:64].astype(jnp.float32), PACKED[level], 1)
        packed = jnp.where(lanes >= PACKED[level], moved, packed)
    queries_ref[...] = packed.astype(jnp.bfloat16)
    ready = []
    for tile in small:
        keys = tile[64:128].astype(jnp.float32)
        values = pltpu.roll(tile[128:].astype(jnp.float32), 64, 1)
        ready.append(jnp.where(lanes < 64, keys, values).astype(jnp.bfloat16))
    for there in range(16):
        level = needed_level(plane, there)
        for at in range(5, 9):

            @pl.when(level == at)
            def _(there=there, at=at):
                far_ref[there] = ready[at - 5]


def needed_level(plane, there):
    level = jnp.int32(8)
    for at in (7, 6, 5):
        near = jnp.abs((plane >> (at - 5)) - (there >> (at - 5))) <= 1
        level = jnp.where(near, jnp.int32(at), level)
    return level


def softmax_parts(parts):
    top = parts[0].max(axis=0, keepdims=True)
    for part in parts[1:]:
        top = jnp.maximum(top, part.max(axis=0, keepdims=True))
    top = top * SCALE
    weights, total = [], None
    for part in parts:
        grown = jnp.exp2(part * SCALE - top)
        added = grown.sum(axis=0, keepdims=True)
        total = added if total is None else total + added
        weights.append(grown.astype(jnp.bfloat16))
    return top, total, weights


def near_tile(query, keys, values, bias=(None, None, None)):
    parts = []
    for key, add in zip(keys, bias):
        scores = mm(key, query)
        parts.append(scores if add is None else scores + add)
    top, total, weights = softmax_parts(parts)
    numer = mm(jnp.concatenate(values, axis=1), jnp.concatenate(weights, axis=0))
    return numer, top, total


def far_tile(query, keys, values, level, bias=(None, None)):
    scores = []
    for key, add in zip(keys, bias):
        part = mm(key, query)
        scores.append(part if add is None else part + add)
    lower = iota((64, 128), 1) < 64
    middle = jnp.where(lower, scores[1][:64], scores[0][64:])
    top, total, weights = softmax_parts([scores[0][:64], middle, scores[1][64:]])
    none = jnp.zeros_like(weights[1])
    spread = [weights[0], jnp.where(lower, none, weights[1]), jnp.where(lower, weights[1], none), weights[2]]
    numer = mm(jnp.concatenate(values, axis=1), jnp.concatenate(spread, axis=0))
    times = 2.0**level
    return numer * times, top, total * times


def put(ref, place, state):
    numer, top, total = state
    ref[place, :64] = numer
    ref[place, 64:65] = top
    ref[place, 65:66] = total


def get(ref, place):
    return ref[place, :64], ref[place, 64:65], ref[place, 65:66]


def merge(one, two):
    top = jnp.maximum(one[1], two[1])
    scale_one = jnp.exp2(one[1] - top)
    scale_two = jnp.exp2(two[1] - top)
    return one[0] * scale_one + two[0] * scale_two, top, one[2] * scale_one + two[2] * scale_two


def lanes_from(state, picks):
    wide = jnp.concatenate([picks] * 8, axis=0)
    both = jnp.concatenate([state[1], state[2], jnp.zeros((6, 128), jnp.float32)], axis=0)
    both = jnp.take_along_axis(both, picks, axis=1)
    return jnp.take_along_axis(state[0], wide, axis=1), both[0:1], both[1:2]


STATE_TILES = TILES + 8 + 4
STATE_AT = {0: 0, 1: 16, 2: 24}


def interior_kernel(x_ref, tiles_ref, state_ref):
    def tile(level, i):
        return x_ref.at[i] if level == 0 else tiles_ref.at[OFFSET[level] + i]

    for level in range(3):
        count = COUNT[level]
        turned = {}
        for i in range(count):
            if level == 0 or 1 <= i + 1 < count or 1 <= i - 1:
                turned[i] = tile(level, i)[64:128].T
        for i in range(1, count - 1):
            query = tile(level, i)[:64]
            at = (i - 1, i, i + 1) if level == 0 else (i - 1, i + 1)
            keys = [turned[n] for n in at]
            values = [tile(level, n)[128:] for n in at]
            state = near_tile(query, keys, values) if level == 0 else far_tile(query, keys, values, level)
            put(state_ref, STATE_AT[level] + i, state)


def edges_kernel(place_ref, x_ref, tiles_ref, before_ref, after_ref, inner_ref, state_ref):
    place = place_ref[0]
    last_place = place_ref[1]
    no_before = jnp.where(place == 0, jnp.float32(NEVER), jnp.float32(0.0))
    no_after = jnp.where(place == last_place, jnp.float32(NEVER), jnp.float32(0.0))
    lanes = iota((8, 128), 1)

    def tile(level, i):
        return x_ref.at[i] if level == 0 else tiles_ref.at[OFFSET[level] + i]

    def side(level, i):
        if i < 0:
            return before_ref[level, :64].T, before_ref[level, 64:], no_before
        if i >= COUNT[level]:
            return after_ref[level, :64].T, after_ref[level, 64:], no_after
        return tile(level, i)[64:128].T, tile(level, i)[128:], None

    coarser = None
    for level in (4, 3, 2, 1, 0):
        merged = []
        for i in range(COUNT[level]):
            if level < 3 and 0 < i < COUNT[level] - 1:
                state = get(inner_ref, STATE_AT[level] + i)
            else:
                at = (i - 1, i, i + 1) if level == 0 else (i - 1, i + 1)
                keys, values, bias = zip(*(side(level, n) for n in at))
                query = tile(level, i)[:64]
                if level == 0:
                    state = near_tile(query, keys, values, bias)
                else:
                    state = far_tile(query, keys, values, level, bias)
            if coarser is not None:
                picks = 64 * (i % 2) + lanes // 2
                state = merge(state, lanes_from(coarser[i // 2], picks))
            merged.append(state)
        coarser = merged
    for i in range(TILES):
        put(state_ref, i, coarser[i])


def final_kernel(place_ref, queries_ref, own_ref, other_ref, state_ref, out_ref, bias_ref):
    plane = place_ref[0] >> 1
    core = place_ref[0] & 1
    query = queries_ref[...]
    lane = iota((32, 128), 1)
    slot = iota((32, 128), 0)
    lane_level = jnp.where(lane < 64, 5, jnp.where(lane < 96, 6, jnp.where(lane < 112, 7, 8)))
    bias_ref[0] = jnp.full((32, 128), NEVER, jnp.float32)
    for level in (6, 7, 8):
        held = (lane_level == level) & (slot < (64 >> (level - 5)))
        bias_ref[level - 5] = jnp.where(held, 0.0, NEVER)

    pick = (iota((128, 512), 0) // 32 == iota((128, 512), 1) // 128) & (
        iota((128, 512), 0) % 32 == iota((128, 512), 1) % 128
    )
    pick = jnp.where(pick, 1.0, 0.0).astype(jnp.bfloat16)
    place_value = (iota((512, 128), 1) // 32 == iota((512, 128), 0) // 128) & (
        iota((512, 128), 1) % 32 + 64 == iota((512, 128), 0) % 128
    )
    place_value = jnp.where(place_value, 1.0, 0.0).astype(jnp.bfloat16)
    parts, values = [], []
    for ref in (own_ref, other_ref):
        for four in range(4):
            chunks = jnp.concatenate([ref[4 * four + n] for n in range(4)], axis=1)
            key = lax.dot_general(
                pick, chunks, (((1,), (1,)), ((), ())), preferred_element_type=jnp.float32
            ).astype(jnp.bfloat16)
            values.append(mm(chunks, place_value).astype(jnp.bfloat16))
            bias = [bias_ref[needed_level(plane, 4 * four + n) - 5] for n in range(4)]
            parts.append(mm(key, query) + jnp.concatenate(bias, axis=0))
    first_lanes = jnp.where(iota((1, 128), 1) < 64, 0.0, NEVER)
    for step in (-1, 1):
        there = plane + step
        held = (there >= 0) & (there < 16)
        at = jnp.clip(there, 0, 15)
        for mine, ref in ((True, own_ref), (False, other_ref)):
            source = core if mine else 1 - core
            apart = 2 * step + source - core
            keep = held & (jnp.abs(apart) >= 2)
            chunk = ref[at]
            turned = chunk.T
            parts.append(mm(turned[:64], query) + (first_lanes + jnp.where(keep, 0.0, NEVER)))
            values.append(chunk[:, 64:])
    top, total, weights = softmax_parts(parts)
    numer = mm(jnp.concatenate(values, axis=1), jnp.concatenate(weights, axis=0))
    row = lane_level[:1]
    times = jnp.where(row == 5, 32.0, jnp.where(row == 6, 64.0, jnp.where(row == 7, 128.0, 256.0)))
    packed = (numer * times, top, total * times)
    lanes = iota((8, 128), 1)
    state = packed
    for level in (6, 7, 8):
        picks = jnp.minimum(PACKED[level] + lanes // (1 << (level - 5)), 127)
        state = merge(state, lanes_from(packed, picks))
    for i in range(TILES):
        spread = lanes_from(state, 4 * i + lanes // 32)
        numer, _, total = merge(get(state_ref, i), spread)
        out_ref[i] = (numer / total).astype(jnp.bfloat16)


def cost(flops, moved, exps=0):
    return pl.CostEstimate(flops=flops, bytes_accessed=moved, transcendentals=exps)


def body(queries, key_rows, value_rows):
    bf16, f32 = jnp.bfloat16, jnp.float32
    outer = lax.axis_size("seqhi")
    place = lax.axis_index("seqhi").astype(jnp.int32)
    place_info = jnp.stack([place, jnp.int32(outer - 1)])
    shape = jax.ShapeDtypeStruct

    split = pl.pallas_call(
        split_kernel,
        out_shape=shape((HEADS, 192, 128), bf16),
        in_specs=[VMEM] * 3,
        out_specs=VMEM,
        compiler_params=PARAMS,
        cost_estimate=cost(1 << 22, 3 << 19),
    )(queries, key_rows, value_rows)
    tokens = lax.all_to_all(split, "seqlo", 0, 0)

    tiles, packed, to_left, to_right, far = pl.pallas_call(
        coarse_kernel,
        out_shape=(
            shape((15, 192, 128), bf16),
            shape((64, 128), bf16),
            shape((5, 128, 128), bf16),
            shape((5, 128, 128), bf16),
            shape((16, 64, 128), bf16),
        ),
        in_specs=[SMEM, VMEM],
        out_specs=(VMEM,) * 5,
        compiler_params=PARAMS,
        cost_estimate=cost(1 << 28, 2 << 20),
    )(place_info[:1] >> 1, tokens)

    planes = [[2 * z + core for z in range(outer // 2)] for core in range(2)]
    own = lax.all_to_all(far, "seqhi", 0, 0, axis_index_groups=planes)
    before = lax.ppermute(to_right, "seqhi", [(i, i + 1) for i in range(outer - 1)])
    after = lax.ppermute(to_left, "seqhi", [(i + 1, i) for i in range(outer - 1)])
    other = lax.ppermute(own, "seqhi", [(i, i ^ 1) for i in range(outer)])

    inner = pl.pallas_call(
        interior_kernel,
        out_shape=shape((STATE_TILES, ROWS, 128), f32),
        in_specs=[VMEM] * 2,
        out_specs=VMEM,
        compiler_params=PARAMS,
        cost_estimate=cost(1 << 32, 2 << 20, 1 << 20),
    )(tokens, tiles)
    local = pl.pallas_call(
        edges_kernel,
        out_shape=shape((TILES, ROWS, 128), f32),
        in_specs=[SMEM] + [VMEM] * 5,
        out_specs=VMEM,
        compiler_params=PARAMS,
        cost_estimate=cost(1 << 31, 2 << 20, 1 << 19),
    )(place_info, tokens, tiles, before, after, inner)
    out = pl.pallas_call(
        final_kernel,
        out_shape=shape((TILES, HEAD, 128), bf16),
        in_specs=[SMEM] + [VMEM] * 4,
        out_specs=VMEM,
        scratch_shapes=[pltpu.VMEM((4, 32, 128), f32)],
        compiler_params=PARAMS,
        cost_estimate=cost(1 << 30, 2 << 20, 1 << 18),
    )(place_info, packed, own, other, local)

    heads = lax.all_to_all(out, "seqlo", 0, 0)
    return pl.pallas_call(
        join_kernel,
        out_shape=shape((128, HEADS * HEAD), bf16),
        in_specs=[VMEM],
        out_specs=VMEM,
        compiler_params=PARAMS,
        cost_estimate=cost(1 << 22, 1 << 19),
    )(heads)


def solution(mesh):
    placed = P(("seqhi", "seqlo"), None)
    return jax.shard_map(body, mesh=mesh, in_specs=(placed,) * 3, out_specs=placed, check_vma=False)
```

```python
import functools
import math

import jax
import jax.numpy as jnp
from jax import lax
from jax.experimental import pallas as pl
from jax.experimental.pallas import tpu as pltpu
from jax.sharding import PartitionSpec as P

HEADS = 16
HEAD = 64
BLOCK = 128
NEVER = -1e30
SCALE = math.log2(math.e) / math.sqrt(HEAD)
TILES = 16
OFFSET = {1: 0, 2: 8, 3: 12, 4: 14}
COUNT = {0: 16, 1: 8, 2: 4, 3: 2, 4: 1}
ROWS = 72
PACKED = {5: 0, 6: 64, 7: 96, 8: 112}

VMEM = pl.BlockSpec(memory_space=pltpu.VMEM)
SMEM = pl.BlockSpec(memory_space=pltpu.SMEM)


def iota(shape, dim):
    return lax.broadcasted_iota(jnp.int32, shape, dim)


def mm(a, b):
    return jnp.dot(a, b, preferred_element_type=jnp.float32)


def split_kernel(count, *refs):
    sources, out_ref, held, sems = refs[:count], refs[count], refs[count + 1], refs[count + 2]
    copies = []
    for place in range(count):
        for part in range(2):
            columns = pl.ds(512 * part, 512)
            copy = pltpu.make_async_copy(
                sources[place].at[:, columns], held.at[place, :, columns], sems.at[place, part]
            )
            copy.start()
            copies.append((place, part, copy))
    for place, part, copy in copies:
        copy.wait()
        for pair in range(4 * part, 4 * part + 4):
            turned = held[place, :, 128 * pair : 128 * pair + 128].T
            out_ref[2 * pair, 64 * place : 64 * place + 64, :] = turned[:64]
            out_ref[2 * pair + 1, 64 * place : 64 * place + 64, :] = turned[64:]


def join_kernel(in_ref, out_ref):
    for pair in range(HEADS // 2):
        both = jnp.concatenate([in_ref[2 * pair], in_ref[2 * pair + 1]], axis=0)
        out_ref[:, 128 * pair : 128 * pair + 128] = both.T


def halving():
    wanted = iota((256, 128), 0) // 2 == iota((256, 128), 1)
    return jnp.where(wanted, 0.5, 0.0).astype(jnp.bfloat16)


def coarser_tiles(finer, halve):
    out = []
    for i in range(len(finer) // 2):
        pair = jnp.concatenate([finer[2 * i], finer[2 * i + 1]], axis=1)
        out.append(mm(pair, halve).astype(jnp.bfloat16))
    return out


def coarse_kernel(place_ref, x_ref, tiles_ref, inside_ref, outside_ref, far_ref, ready_ref):
    plane = place_ref[0] >> 1
    first_core = (place_ref[0] & 1) == 0
    halve = halving()
    finer = [x_ref[i, :128] for i in range(TILES)]
    ends = [(finer[0], finer[-1])]
    for level in range(1, 5):
        finer = coarser_tiles(finer, halve)
        for i, tile in enumerate(finer):
            tiles_ref[OFFSET[level] + i] = tile
        ends.append((finer[0], finer[-1]))
    tile = finer[0]
    lanes = iota((64, 128), 1)
    for level in range(5, 9):
        tile = mm(tile, halve[:128]).astype(jnp.bfloat16)
        values = pltpu.roll(tile[64:].astype(jnp.float32), 64, 1)
        ready_ref[level - 5] = jnp.where(lanes < 64, tile[:64].astype(jnp.float32), values).astype(jnp.bfloat16)
    for there in range(16):
        far_ref[there] = ready_ref[needed_level(plane, there) - 5]
    for level, (first, last) in enumerate(ends):
        inside_ref[level] = jnp.where(first_core, last, first)
        outside_ref[level] = jnp.where(first_core, first, last)


def needed_level(plane, there):
    level = jnp.int32(8)
    for at in (7, 6, 5):
        near = jnp.abs((plane >> (at - 5)) - (there >> (at - 5))) <= 1
        level = jnp.where(near, jnp.int32(at), level)
    return level


def softmax_parts(parts):
    top = parts[0].max(axis=0, keepdims=True)
    for part in parts[1:]:
        top = jnp.maximum(top, part.max(axis=0, keepdims=True))
    top = top * SCALE
    weights, total = [], None
    for part in parts:
        grown = jnp.exp2(part * SCALE - top)
        added = grown.sum(axis=0, keepdims=True)
        total = added if total is None else total + added
        weights.append(grown.astype(jnp.bfloat16))
    return top, total, weights


def near_tile(query, keys, values, bias=(None, None, None)):
    parts = []
    for key, add in zip(keys, bias):
        scores = mm(key, query)
        parts.append(scores if add is None else scores + add)
    top, total, weights = softmax_parts(parts)
    numer = mm(jnp.concatenate(values, axis=1), jnp.concatenate(weights, axis=0))
    return numer, top, total


def far_tile(query, keys, values, level, bias=(None, None)):
    scores = []
    for key, add in zip(keys, bias):
        part = mm(key, query)
        scores.append(part if add is None else part + add)
    lower = iota((64, 128), 1) < 64
    middle = jnp.where(lower, scores[1][:64], scores[0][64:])
    top, total, weights = softmax_parts([scores[0][:64], middle, scores[1][64:]])
    none = jnp.zeros_like(weights[1])
    spread = [weights[0], jnp.where(lower, none, weights[1]), jnp.where(lower, weights[1], none), weights[2]]
    numer = mm(jnp.concatenate(values, axis=1), jnp.concatenate(spread, axis=0))
    times = 2.0**level
    return numer * times, top, total * times


def put(ref, place, state):
    numer, top, total = state
    ref[place, :64] = numer
    ref[place, 64:65] = top
    ref[place, 65:66] = total


def get(ref, place):
    return ref[place, :64], ref[place, 64:65], ref[place, 65:66]


def merge(one, two):
    top = jnp.maximum(one[1], two[1])
    scale_one = jnp.exp2(one[1] - top)
    scale_two = jnp.exp2(two[1] - top)
    return one[0] * scale_one + two[0] * scale_two, top, one[2] * scale_one + two[2] * scale_two


def lanes_from(state, picks):
    wide = jnp.concatenate([picks] * 8, axis=0)
    both = jnp.concatenate([state[1], state[2], jnp.zeros((6, 128), jnp.float32)], axis=0)
    both = jnp.take_along_axis(both, picks, axis=1)
    return jnp.take_along_axis(state[0], wide, axis=1), both[0:1], both[1:2]


STATE_TILES = TILES + 8 + 4
STATE_AT = {0: 0, 1: 16, 2: 24}


def level_tile(level_zero, coarse, level, i):
    return level_zero.at[i] if level == 0 else coarse.at[OFFSET[level] + i]


def query_tile(level_zero, coarse, level, i):
    return level_zero[i, 128:] if level == 0 else coarse[OFFSET[level] + i]


def interior_kernel(x_ref, tiles_ref, state_ref, coarse_q_ref, packed_ref):
    halve = halving()
    finer = [x_ref[i, 128:] for i in range(TILES)]
    for level in range(1, 5):
        finer = coarser_tiles(finer, halve)
        for i, tile in enumerate(finer):
            coarse_q_ref[OFFSET[level] + i] = tile
    tile, packed = finer[0], None
    lanes = iota((64, 128), 1)
    for level in range(5, 9):
        tile = mm(tile, halve[:128]).astype(jnp.bfloat16)
        wide = tile.astype(jnp.float32)
        if level == 5:
            packed = wide
        else:
            packed = jnp.where(lanes >= PACKED[level], pltpu.roll(wide, PACKED[level], 1), packed)
    packed_ref[...] = packed.astype(jnp.bfloat16)

    for level in range(3):
        count = COUNT[level]
        turned = {}
        for i in range(1, count - 1):
            query = query_tile(x_ref, coarse_q_ref, level, i)
            at = (i - 1, i, i + 1) if level == 0 else (i - 1, i + 1)
            for n in at:
                if n not in turned:
                    turned[n] = level_tile(x_ref, tiles_ref, level, n)[:64].T
            keys = [turned[n] for n in at]
            values = [level_tile(x_ref, tiles_ref, level, n)[64:128] for n in at]
            state = near_tile(query, keys, values) if level == 0 else far_tile(query, keys, values, level)
            put(state_ref, STATE_AT[level] + i, state)


def edges_kernel(place_ref, coarse_q_ref, x_ref, tiles_ref, inside_ref, outside_ref, inner_ref, state_ref):
    place = place_ref[0]
    last_place = place_ref[1]
    first_core = (place & 1) == 0
    no_before = jnp.where(place == 0, jnp.float32(NEVER), jnp.float32(0.0))
    no_after = jnp.where(place == last_place, jnp.float32(NEVER), jnp.float32(0.0))
    lanes = iota((8, 128), 1)

    def side(level, i):
        if 0 <= i < COUNT[level]:
            ref = level_tile(x_ref, tiles_ref, level, i)
            return ref[:64].T, ref[64:128], None
        came_inside = first_core if i >= 0 else jnp.logical_not(first_core)
        both = jnp.where(came_inside, inside_ref[level], outside_ref[level])
        return both[:64].T, both[64:], no_before if i < 0 else no_after

    coarser = None
    for level in (4, 3, 2, 1, 0):
        merged = []
        for i in range(COUNT[level]):
            if level < 3 and 0 < i < COUNT[level] - 1:
                state = get(inner_ref, STATE_AT[level] + i)
            else:
                at = (i - 1, i, i + 1) if level == 0 else (i - 1, i + 1)
                keys, values, bias = zip(*(side(level, n) for n in at))
                query = query_tile(x_ref, coarse_q_ref, level, i)
                if level == 0:
                    state = near_tile(query, keys, values, bias)
                else:
                    state = far_tile(query, keys, values, level, bias)
            if coarser is not None:
                picks = 64 * (i % 2) + lanes // 2
                state = merge(state, lanes_from(coarser[i // 2], picks))
            merged.append(state)
        coarser = merged
    for i in range(TILES):
        put(state_ref, i, coarser[i])


def lane_levels():
    lane = iota((32, 128), 1)
    return jnp.where(lane < 64, 5, jnp.where(lane < 96, 6, jnp.where(lane < 112, 7, 8)))


def far_state(plane, core, source, query, ref, bias_ref):
    slot = iota((32, 128), 0)
    lane_level = lane_levels()
    bias_ref[0] = jnp.full((32, 128), NEVER, jnp.float32)
    for level in (6, 7, 8):
        held = (lane_level == level) & (slot < (64 >> (level - 5)))
        bias_ref[level - 5] = jnp.where(held, 0.0, NEVER)

    rows, lanes = iota((128, 512), 0), iota((128, 512), 1)
    pick = jnp.where((rows // 32 == lanes // 128) & (rows % 32 == lanes % 128), 1.0, 0.0).astype(jnp.bfloat16)
    rows, lanes = iota((512, 128), 0), iota((512, 128), 1)
    place = (lanes // 32 == rows // 128) & (lanes % 32 + 64 == rows % 128)
    place = jnp.where(place, 1.0, 0.0).astype(jnp.bfloat16)
    parts, values = [], []
    for four in range(4):
        chunks = jnp.concatenate([ref[4 * four + n] for n in range(4)], axis=1)
        key = lax.dot_general(
            pick, chunks, (((1,), (1,)), ((), ())), preferred_element_type=jnp.float32
        ).astype(jnp.bfloat16)
        values.append(mm(chunks, place).astype(jnp.bfloat16))
        bias = [bias_ref[needed_level(plane, 4 * four + n) - 5] for n in range(4)]
        parts.append(mm(key, query) + jnp.concatenate(bias, axis=0))
    first_lanes = jnp.where(iota((1, 128), 1) < 64, 0.0, NEVER)
    for step in (-1, 1):
        there = plane + step
        held = (there >= 0) & (there < 16) & (jnp.abs(2 * step + source - core) >= 2)
        chunk = ref[jnp.clip(there, 0, 15)]
        turned = chunk.T
        parts.append(mm(turned[:64], query) + (first_lanes + jnp.where(held, 0.0, NEVER)))
        values.append(chunk[:, 64:])
    top, total, weights = softmax_parts(parts)
    return mm(jnp.concatenate(values, axis=1), jnp.concatenate(weights, axis=0)), top, total


def own_kernel(place_ref, packed_ref, chunks_ref, state_ref, bias_ref):
    plane, core = place_ref[0] >> 1, place_ref[0] & 1
    put(state_ref, 0, far_state(plane, core, core, packed_ref[...], chunks_ref, bias_ref))


def final_kernel(place_ref, packed_ref, chunks_ref, own_ref, local_ref, out_ref, bias_ref):
    plane, core = place_ref[0] >> 1, place_ref[0] & 1
    state = far_state(plane, core, 1 - core, packed_ref[...], chunks_ref, bias_ref)
    numer, top, total = merge(state, get(own_ref, 0))
    row = lane_levels()[:1]
    times = jnp.where(row == 5, 32.0, jnp.where(row == 6, 64.0, jnp.where(row == 7, 128.0, 256.0)))
    packed = (numer * times, top, total * times)
    lanes = iota((8, 128), 1)
    state = packed
    for level in (6, 7, 8):
        picks = jnp.minimum(PACKED[level] + lanes // (1 << (level - 5)), 127)
        state = merge(state, lanes_from(packed, picks))
    for i in range(TILES):
        spread = lanes_from(state, 4 * i + lanes // 32)
        numer, _, total = merge(get(local_ref, i), spread)
        out_ref[i] = (numer / total).astype(jnp.bfloat16)


def call(kernel, out_shape, in_specs, flops, moved, exps=0, scratch=(), limit=48):
    out_specs = (VMEM,) * len(out_shape) if isinstance(out_shape, tuple) else VMEM
    return pl.pallas_call(
        kernel,
        out_shape=out_shape,
        in_specs=in_specs,
        out_specs=out_specs,
        scratch_shapes=scratch,
        compiler_params=pltpu.CompilerParams(vmem_limit_bytes=limit << 20),
        cost_estimate=pl.CostEstimate(flops=flops, bytes_accessed=moved, transcendentals=exps),
    )


def split(*arrays):
    count = len(arrays)
    return call(
        functools.partial(split_kernel, count),
        jax.ShapeDtypeStruct((HEADS, 64 * count, 128), jnp.bfloat16),
        [pl.BlockSpec(memory_space=pltpu.HBM)] * count,
        1 << 22,
        count << 19,
        scratch=[pltpu.VMEM((count, 128, HEADS * HEAD), jnp.bfloat16), pltpu.SemaphoreType.DMA((count, 2))],
        limit=62,
    )(*arrays)


def body(queries, key_rows, value_rows):
    bf16, f32 = jnp.bfloat16, jnp.float32
    outer = lax.axis_size("seqhi")
    place = lax.axis_index("seqhi").astype(jnp.int32)
    place_info = jnp.stack([place, jnp.int32(outer - 1)])
    shape = jax.ShapeDtypeStruct

    tokens = lax.all_to_all(split(key_rows, value_rows, queries), "seqlo", 0, 0)

    tiles, inside, outside, far = call(
        coarse_kernel,
        (
            shape((15, 128, 128), bf16),
            shape((5, 128, 128), bf16),
            shape((5, 128, 128), bf16),
            shape((16, 64, 128), bf16),
        ),
        [SMEM, VMEM],
        1 << 27,
        2 << 20,
        scratch=[pltpu.VMEM((4, 64, 128), bf16)],
    )(place_info, tokens)

    planes = [[2 * z + core for z in range(outer // 2)] for core in range(2)]
    own = lax.all_to_all(far, "seqhi", 0, 0, axis_index_groups=planes)
    cores = [(i, i ^ 1) for i in range(outer)]
    inside = lax.ppermute(inside, "seqhi", cores)
    beside = [pair for i in range(1, outer - 1, 2) for pair in ((i, i + 1), (i + 1, i))]
    outside = lax.ppermute(outside, "seqhi", beside)

    inner, coarse_q, packed = call(
        interior_kernel,
        (shape((STATE_TILES, ROWS, 128), f32), shape((15, 64, 128), bf16), shape((64, 128), bf16)),
        [VMEM] * 2,
        1 << 32,
        2 << 20,
        1 << 20,
    )(tokens, tiles)
    local = call(
        edges_kernel, shape((TILES, ROWS, 128), f32), [SMEM] + [VMEM] * 6, 1 << 31, 2 << 20, 1 << 19
    )(place_info, coarse_q, tokens, tiles, inside, outside, inner)

    own, local = lax.optimization_barrier((own, local))
    other = lax.ppermute(own, "seqhi", cores)
    bias = pltpu.VMEM((4, 32, 128), f32)
    own_state = call(
        own_kernel, shape((1, ROWS, 128), f32), [SMEM] + [VMEM] * 2, 1 << 30, 1 << 20, 1 << 17, [bias]
    )(place_info, packed, own)
    out = call(
        final_kernel, shape((TILES, HEAD, 128), bf16), [SMEM] + [VMEM] * 4, 1 << 30, 2 << 20, 1 << 17, [bias]
    )(place_info, packed, other, own_state, local)

    heads = lax.all_to_all(out, "seqlo", 0, 0)
    return call(join_kernel, shape((128, HEADS * HEAD), bf16), [VMEM], 1 << 22, 1 << 19)(heads)


def solution(mesh):
    placed = P(("seqhi", "seqlo"), None)
    return jax.shard_map(body, mesh=mesh, in_specs=(placed,) * 3, out_specs=placed, check_vma=False)
```

```python
import functools
import math

import jax
import jax.numpy as jnp
from jax import lax
from jax.experimental import pallas as pl
from jax.experimental.pallas import tpu as pltpu
from jax.sharding import PartitionSpec as P

HEADS = 16
HEAD = 64
BLOCK = 128
NEVER = -1e30
SCALE = math.log2(math.e) / math.sqrt(HEAD)
TILES = 16
OFFSET = {1: 0, 2: 8, 3: 12, 4: 14}
COUNT = {0: 16, 1: 8, 2: 4, 3: 2, 4: 1}
ROWS = 72
PACKED = {5: 0, 6: 64, 7: 96, 8: 112}

VMEM = pl.BlockSpec(memory_space=pltpu.VMEM)


def iota(shape, dim):
    return lax.broadcasted_iota(jnp.int32, shape, dim)


def mm(a, b):
    return jnp.dot(a, b, preferred_element_type=jnp.float32)


def split_kernel(count, *refs):
    sources, out_ref, held, sems = refs[:count], refs[count], refs[count + 1], refs[count + 2]
    copies = []
    for place in range(count):
        for part in range(2):
            columns = pl.ds(512 * part, 512)
            copy = pltpu.make_async_copy(
                sources[place].at[:, columns], held.at[place, :, columns], sems.at[place, part]
            )
            copy.start()
            copies.append((place, part, copy))
    for place, part, copy in copies:
        copy.wait()
        for pair in range(4 * part, 4 * part + 4):
            turned = held[place, :, 128 * pair : 128 * pair + 128].T
            out_ref[2 * pair, 64 * place : 64 * place + 64, :] = turned[:64]
            out_ref[2 * pair + 1, 64 * place : 64 * place + 64, :] = turned[64:]


def join_kernel(in_ref, out_ref):
    for pair in range(HEADS // 2):
        both = jnp.concatenate([in_ref[2 * pair], in_ref[2 * pair + 1]], axis=0)
        out_ref[:, 128 * pair : 128 * pair + 128] = both.T


def halving():
    wanted = iota((256, 128), 0) // 2 == iota((256, 128), 1)
    return jnp.where(wanted, 0.5, 0.0).astype(jnp.bfloat16)


def halving_rows(rows, columns):
    return jnp.where(iota((rows, columns), 1) // 2 == iota((rows, columns), 0), 0.5, 0.0).astype(jnp.bfloat16)


def coarser_tiles(finer, halve):
    count, dims = len(finer) // 2, finer[0].shape[0]
    pairs = [jnp.concatenate([finer[2 * i], finer[2 * i + 1]], axis=1) for i in range(count)]
    joined = mm(jnp.concatenate(pairs, axis=0), halve).astype(jnp.bfloat16)
    return [joined[dims * i : dims * (i + 1)] for i in range(count)]


def coarse_kernel(x_ref, far_ref, fifth_ref, tiles_ref, ready_ref):
    place = lax.axis_index("seqhi")
    plane = place >> 1
    halve = halving()
    finer = [x_ref[i, :128] for i in range(TILES)]
    for level in range(1, 5):
        finer = coarser_tiles(finer, halve)
        for i, tile in enumerate(finer):
            tiles_ref[OFFSET[level] + i] = tile
    fifth = lax.dot_general(
        halving_rows(64, 128), finer[0], (((1,), (1,)), ((), ())), preferred_element_type=jnp.float32
    ).astype(jnp.bfloat16)
    fifth_ref[...] = fifth
    finer = fifth
    ready_ref[0] = jnp.zeros((32, 128), jnp.bfloat16)
    for level in (6, 7, 8):
        finer = mm(halving_rows(32, finer.shape[0]), finer).astype(jnp.bfloat16)
        ready_ref[level - 5] = finer
    for there in range(16):
        far_ref[there] = ready_ref[needed_level(plane, there) - 5]


def needed_level(plane, there):
    level = jnp.int32(8)
    for at in (7, 6, 5):
        near = jnp.abs((plane >> (at - 5)) - (there >> (at - 5))) <= 1
        level = jnp.where(near, jnp.int32(at), level)
    return level


class Task:
    def __init__(self, level, query, keys, values, bias=None):
        self.level, self.query, self.keys, self.values = level, query, keys, values
        self.bias = bias or [None] * len(keys)
        self.rows = 128 * len(keys)


def biased(scores, add):
    return scores if add is None else scores + add


def softmax_parts(parts):
    top = parts[0].max(axis=0, keepdims=True)
    for part in parts[1:]:
        top = jnp.maximum(top, part.max(axis=0, keepdims=True))
    top = top * SCALE
    weights, total = [], None
    for part in parts:
        grown = jnp.exp2(part * SCALE - top)
        added = grown.sum(axis=0, keepdims=True)
        total = added if total is None else total + added
        weights.append(grown.astype(jnp.bfloat16))
    return top, total, weights


def attend_all(tasks, score_ref, weight_ref):
    lower = iota((64, 128), 1) < 64
    none = jnp.zeros((64, 128), jnp.bfloat16)
    for n, task in enumerate(tasks):
        score_ref[n, : task.rows] = mm(jnp.concatenate(task.keys, axis=0), task.query)
    tops = []
    for n, task in enumerate(tasks):
        if task.level == 0:
            parts = [biased(score_ref[n, 128 * i : 128 * i + 128], add) for i, add in enumerate(task.bias)]
            top, total, weights = softmax_parts(parts)
            for i, weight in enumerate(weights):
                weight_ref[n, 128 * i : 128 * i + 128] = weight
        else:
            first, second, third, fourth = (
                biased(score_ref[n, 64 * i : 64 * i + 64], task.bias[i // 2]) for i in range(4)
            )
            top, total, weights = softmax_parts([first, jnp.where(lower, third, second), fourth])
            weight_ref[n, 0:64] = weights[0]
            weight_ref[n, 64:128] = jnp.where(lower, none, weights[1])
            weight_ref[n, 128:192] = jnp.where(lower, weights[1], none)
            weight_ref[n, 192:256] = weights[2]
        tops.append((top, total))
    states = []
    for n, task in enumerate(tasks):
        numer = mm(jnp.concatenate(task.values, axis=1), weight_ref[n, : task.rows])
        times = 2.0**task.level
        top, total = tops[n]
        states.append((numer * times, top, total * times) if task.level else (numer, top, total))
    return states


def put(ref, place, state):
    numer, top, total = state
    ref[place, :64] = numer
    ref[place, 64:65] = top
    ref[place, 65:66] = total


def get(ref, place):
    return ref[place, :64], ref[place, 64:65], ref[place, 65:66]


def merge(one, two):
    top = jnp.maximum(one[1], two[1])
    scale_one = jnp.exp2(one[1] - top)
    scale_two = jnp.exp2(two[1] - top)
    return one[0] * scale_one + two[0] * scale_two, top, one[2] * scale_one + two[2] * scale_two


def lanes_from(state, picks):
    wide = jnp.concatenate([picks] * 8, axis=0)
    both = jnp.concatenate([state[1], state[2], jnp.zeros((6, 128), jnp.float32)], axis=0)
    both = jnp.take_along_axis(both, picks, axis=1)
    return jnp.take_along_axis(state[0], wide, axis=1), both[0:1], both[1:2]


STATE_TILES = TILES + 8 + 4
STATE_AT = {0: 0, 1: 16, 2: 24}


def level_tile(level_zero, coarse, level, i):
    return level_zero.at[i] if level == 0 else coarse.at[OFFSET[level] + i]


def query_tile(level_zero, coarse, level, i):
    return level_zero[i, 128:] if level == 0 else coarse[OFFSET[level] + i]


def interior_kernel(
    x_ref, tiles_ref, fifth_ref, state_ref, coarse_q_ref, packed_ref, inside_ref, outside_ref, score_ref, weight_ref
):
    first_core = (lax.axis_index("seqhi") & 1) == 0
    for level in range(5):
        first = level_tile(x_ref, tiles_ref, level, 0)[:128]
        last = level_tile(x_ref, tiles_ref, level, COUNT[level] - 1)[:128]
        inside_ref[level] = jnp.where(first_core, last, first)
        sent = jnp.where(first_core, first, last)
        outside_ref[2 * level] = sent[:64]
        outside_ref[2 * level + 1] = sent[64:]
    outside_ref[10] = fifth_ref[...]
    halve = halving()
    finer = [x_ref[i, 128:] for i in range(TILES)]
    for level in range(1, 5):
        finer = coarser_tiles(finer, halve)
        for i, tile in enumerate(finer):
            coarse_q_ref[OFFSET[level] + i] = tile
    tile, packed = finer[0], None
    lanes = iota((64, 128), 1)
    for level in range(5, 9):
        tile = mm(tile, halve[:128]).astype(jnp.bfloat16)
        wide = tile.astype(jnp.float32)
        if level == 5:
            packed = wide
        else:
            packed = jnp.where(lanes >= PACKED[level], pltpu.roll(wide, PACKED[level], 1), packed)
    packed_ref[...] = packed.astype(jnp.bfloat16)

    tasks, places = [], []
    for level in range(3):
        turned = [level_tile(x_ref, tiles_ref, level, n)[:64].T for n in range(COUNT[level])]
        for i in range(1, COUNT[level] - 1):
            at = (i - 1, i, i + 1) if level == 0 else (i - 1, i + 1)
            values = [level_tile(x_ref, tiles_ref, level, n)[64:128] for n in at]
            tasks.append(Task(level, query_tile(x_ref, coarse_q_ref, level, i), [turned[n] for n in at], values))
            places.append(STATE_AT[level] + i)
    for place, state in zip(places, attend_all(tasks, score_ref, weight_ref)):
        put(state_ref, place, state)


def edges_kernel(
    coarse_q_ref, x_ref, tiles_ref, inside_ref, outside_ref, inner_ref, state_ref, score_ref, weight_ref
):
    place = lax.axis_index("seqhi")
    last_place = lax.axis_size("seqhi") - 1
    first_core = (place & 1) == 0
    no_before = jnp.where(place == 0, jnp.float32(NEVER), jnp.float32(0.0))
    no_after = jnp.where(place == last_place, jnp.float32(NEVER), jnp.float32(0.0))
    lanes = iota((8, 128), 1)

    def side(level, i):
        if 0 <= i < COUNT[level]:
            ref = level_tile(x_ref, tiles_ref, level, i)
            return ref[:64].T, ref[64:128], None
        came_inside = first_core if i >= 0 else jnp.logical_not(first_core)
        key = jnp.where(came_inside, inside_ref[level, :64], outside_ref[2 * level])
        value = jnp.where(came_inside, inside_ref[level, 64:], outside_ref[2 * level + 1])
        return key.T, value, no_before if i < 0 else no_after

    tasks, places = [], []
    for level in (4, 3, 2, 1, 0):
        for i in range(COUNT[level]):
            if level < 3 and 0 < i < COUNT[level] - 1:
                continue
            at = (i - 1, i, i + 1) if level == 0 else (i - 1, i + 1)
            keys, values, bias = zip(*(side(level, n) for n in at))
            tasks.append(Task(level, query_tile(x_ref, coarse_q_ref, level, i), keys, values, bias))
            places.append((level, i))
    done = dict(zip(places, attend_all(tasks, score_ref, weight_ref)))
    coarser = None
    for level in (4, 3, 2, 1, 0):
        merged = []
        for i in range(COUNT[level]):
            state = done[level, i] if (level, i) in done else get(inner_ref, STATE_AT[level] + i)
            if coarser is not None:
                state = merge(state, lanes_from(coarser[i // 2], 64 * (i % 2) + lanes // 2))
            merged.append(state)
        coarser = merged
    for i in range(TILES):
        put(state_ref, i, coarser[i])


def lane_levels():
    lane = iota((32, 128), 1)
    return jnp.where(lane < 64, 5, jnp.where(lane < 96, 6, jnp.where(lane < 112, 7, 8)))


def far_state(plane, query, chunks_ref, near, bias_ref, score_ref):
    slot = iota((32, 128), 0)
    lane_level = lane_levels()
    bias_ref[0] = jnp.full((32, 128), NEVER, jnp.float32)
    for level in (6, 7, 8):
        held = (lane_level == level) & (slot < (64 >> (level - 5)))
        bias_ref[level - 5] = jnp.where(held, 0.0, NEVER)
    first_lanes = jnp.where(iota((1, 128), 1) < 64, 0.0, NEVER)
    tall = jnp.concatenate([query, jnp.zeros((64, 128), jnp.bfloat16)], axis=0)
    rows = jnp.concatenate([chunks_ref[...]] + [tile for tile, _ in near], axis=0)
    count = rows.shape[0]
    score_ref[:count] = mm(rows, tall)
    top = None
    for n in range(16 + 2 * len(near)):
        if n < 16:
            bias = bias_ref[needed_level(plane, n) - 5]
        else:
            bias = first_lanes + jnp.where(near[(n - 16) // 2][1], 0.0, NEVER)
        part = score_ref[32 * n : 32 * n + 32] + bias
        score_ref[32 * n : 32 * n + 32] = part
        high = part.max(axis=0, keepdims=True)
        top = high if top is None else jnp.maximum(top, high)
    top = top * SCALE
    grown = jnp.exp2(score_ref[:count] * SCALE - top)
    total = grown.sum(axis=0, keepdims=True)
    both = lax.dot_general(
        rows, grown.astype(jnp.bfloat16), (((0,), (0,)), ((), ())), preferred_element_type=jnp.float32
    )
    return both[64:], top, total


def own_kernel(packed_ref, chunks_ref, beyond_ref, state_ref, bias_ref, score_ref):
    place = lax.axis_index("seqhi")
    toward = jnp.where((place & 1) == 0, place - 2, place + 2)
    near = [(beyond_ref[...], (toward >= 0) & (toward < lax.axis_size("seqhi")))]
    put(state_ref, 0, far_state(place >> 1, packed_ref[...], chunks_ref, near, bias_ref, score_ref))


def final_kernel(packed_ref, other_ref, own_ref, local_ref, out_ref, bias_ref, score_ref):
    place = lax.axis_index("seqhi")
    toward = jnp.where((place & 1) == 0, place + 2, place - 2)
    here = (toward >= 0) & (toward < lax.axis_size("seqhi"))
    near = [(other_ref[512:576], here), (other_ref[576:], here)]
    state = far_state(place >> 1, packed_ref[...], other_ref.at[:512], near, bias_ref, score_ref)
    numer, top, total = merge(state, get(own_ref, 0))
    row = lane_levels()[:1]
    times = jnp.where(row == 5, 32.0, jnp.where(row == 6, 64.0, jnp.where(row == 7, 128.0, 256.0)))
    packed = (numer * times, top, total * times)
    lanes = iota((8, 128), 1)
    state = packed
    for level in (6, 7, 8):
        picks = jnp.minimum(PACKED[level] + lanes // (1 << (level - 5)), 127)
        state = merge(state, lanes_from(packed, picks))
    for i in range(TILES):
        spread = lanes_from(state, 4 * i + lanes // 32)
        numer, _, total = merge(get(local_ref, i), spread)
        out_ref[i] = (numer / total).astype(jnp.bfloat16)


def call(kernel, out_shape, in_specs, flops, moved, exps=0, scratch=(), limit=24):
    out_specs = (VMEM,) * len(out_shape) if isinstance(out_shape, tuple) else VMEM
    return pl.pallas_call(
        kernel,
        out_shape=out_shape,
        in_specs=in_specs,
        out_specs=out_specs,
        scratch_shapes=scratch,
        compiler_params=pltpu.CompilerParams(vmem_limit_bytes=limit << 20),
        cost_estimate=pl.CostEstimate(flops=flops, bytes_accessed=moved, transcendentals=exps),
    )


def split(*arrays):
    count = len(arrays)
    return call(
        functools.partial(split_kernel, count),
        jax.ShapeDtypeStruct((HEADS, 64 * count, 128), jnp.bfloat16),
        [pl.BlockSpec(memory_space=pltpu.HBM)] * count,
        1 << 22,
        count << 19,
        scratch=[pltpu.VMEM((count, 128, HEADS * HEAD), jnp.bfloat16), pltpu.SemaphoreType.DMA((count, 2))],
        limit=62,
    )(*arrays)


def body(queries, key_rows, value_rows):
    bf16, f32 = jnp.bfloat16, jnp.float32
    outer = lax.axis_size("seqhi")
    shape = jax.ShapeDtypeStruct

    tokens = lax.all_to_all(split(key_rows, value_rows, queries), "seqlo", 0, 0)

    far, fifth, tiles = call(
        coarse_kernel,
        (shape((16, 32, 128), bf16), shape((64, 128), bf16), shape((15, 128, 128), bf16)),
        [VMEM],
        1 << 27,
        2 << 20,
        scratch=[pltpu.VMEM((4, 32, 128), bf16)],
    )(tokens)

    planes = [[2 * z + core for z in range(outer // 2)] for core in range(2)]
    own = lax.all_to_all(far, "seqhi", 0, 0, axis_index_groups=planes)
    inner, coarse_q, packed, inside, outside = call(
        interior_kernel,
        (
            shape((STATE_TILES, ROWS, 128), f32),
            shape((15, 64, 128), bf16),
            shape((64, 128), bf16),
            shape((5, 128, 128), bf16),
            shape((11, 64, 128), bf16),
        ),
        [VMEM] * 3,
        1 << 20,
        1 << 16,
        1 << 10,
        [pltpu.VMEM((22, 384, 128), f32), pltpu.VMEM((22, 384, 128), bf16)],
    )(tokens, tiles, fifth)
    beside = [pair for i in range(1, outer - 1, 2) for pair in ((i, i + 1), (i + 1, i))]
    outside = lax.ppermute(outside, "seqhi", beside)
    cores = [(i, i ^ 1) for i in range(outer)]
    inside = lax.ppermute(inside, "seqhi", cores)
    apart = [(i, i + 2) for i in range(0, outer - 2, 2)] + [(i, i - 2) for i in range(3, outer, 2)]
    fifth, inner = lax.optimization_barrier((fifth, inner))
    beyond = lax.ppermute(fifth, "seqhi", apart)
    local = call(
        edges_kernel,
        shape((TILES, ROWS, 128), f32),
        [VMEM] * 6,
        1 << 20,
        1 << 16,
        1 << 10,
        [pltpu.VMEM((9, 384, 128), f32), pltpu.VMEM((9, 384, 128), bf16)],
    )(coarse_q, tokens, tiles, inside, outside, inner)

    own, local = lax.optimization_barrier((own, local))
    own = own.reshape(512, 128)
    other = lax.ppermute(jnp.concatenate([own, outside[10], beyond], axis=0), "seqhi", cores)
    scratch = [pltpu.VMEM((4, 32, 128), f32), pltpu.VMEM((640, 128), f32)]
    own_state = call(
        own_kernel, shape((1, ROWS, 128), f32), [VMEM] * 3, 1 << 30, 1 << 20, 1 << 17, scratch
    )(packed, own, beyond)
    out = call(
        final_kernel, shape((TILES, HEAD, 128), bf16), [VMEM] * 4, 1 << 30, 2 << 20, 1 << 17, scratch
    )(packed, other, own_state, local)

    heads = lax.all_to_all(out, "seqlo", 0, 0)
    return call(join_kernel, shape((128, HEADS * HEAD), bf16), [VMEM], 1 << 22, 1 << 19)(heads)


def solution(mesh):
    placed = P(("seqhi", "seqlo"), None)
    return jax.shard_map(body, mesh=mesh, in_specs=(placed,) * 3, out_specs=placed, check_vma=False)
```

```python
import math

import jax
import jax.numpy as jnp
from jax import lax
from jax.experimental import pallas as pl
from jax.experimental.pallas import tpu as pltpu
from jax.sharding import PartitionSpec as P

HEADS = 16
HEAD = 64
BLOCK = 128
NEVER = -1e30
SCALE = math.log2(math.e) / math.sqrt(HEAD)
TILES = 16
OFFSET = {1: 0, 2: 8, 3: 12, 4: 14}
COUNT = {0: 16, 1: 8, 2: 4, 3: 2, 4: 1}
ROWS = 72
PACKED = {5: 0, 6: 64, 7: 96, 8: 112}

VMEM = pl.BlockSpec(memory_space=pltpu.VMEM)


def iota(shape, dim):
    return lax.broadcasted_iota(jnp.int32, shape, dim)


def mm(a, b):
    return jnp.dot(a, b, preferred_element_type=jnp.float32)


def split_kernel(k_ref, v_ref, q_ref, out_ref, held, turned, in_sems, out_sems):
    copies = [pltpu.make_async_copy(ref, held.at[n], in_sems.at[n]) for n, ref in enumerate((k_ref, v_ref, q_ref))]
    for copy in copies:
        copy.start()
    sent = []
    for n, copy in enumerate(copies):
        copy.wait()
        rows = pl.ds(64 * n, 64)
        for pair in range(HEADS // 2):
            both = held[n, :, 128 * pair : 128 * pair + 128].T
            turned[2 * pair, rows, :] = both[:64]
            turned[2 * pair + 1, rows, :] = both[64:]
        out = pltpu.make_async_copy(turned.at[:, rows], out_ref.at[:, rows], out_sems.at[n])
        out.start()
        sent.append(out)
    for out in sent:
        out.wait()


def join_kernel(in_ref, out_ref):
    for pair in range(HEADS // 2):
        both = jnp.concatenate([in_ref[2 * pair], in_ref[2 * pair + 1]], axis=0)
        out_ref[:, 128 * pair : 128 * pair + 128] = both.T


def halving():
    wanted = iota((256, 128), 0) // 2 == iota((256, 128), 1)
    return jnp.where(wanted, 0.5, 0.0).astype(jnp.bfloat16)


def halving_rows(rows, columns):
    return jnp.where(iota((rows, columns), 1) // 2 == iota((rows, columns), 0), 0.5, 0.0).astype(jnp.bfloat16)


def coarser_tiles(finer, halve):
    pairs = [jnp.concatenate([finer[i], finer[i + 1]], axis=1) for i in range(0, len(finer), 2)]
    return [mm(pair, halve).astype(jnp.bfloat16) for pair in pairs]


def coarse_kernel(x_ref, far_ref, fifth_ref, tiles_ref, ready_ref):
    place = lax.axis_index("seqhi")
    plane = place >> 1
    halve = halving()
    finer = [x_ref[i, :128] for i in range(TILES)]
    for level in range(1, 5):
        finer = coarser_tiles(finer, halve)
        for i, tile in enumerate(finer):
            tiles_ref[OFFSET[level] + i] = tile
    fifth = lax.dot_general(
        halving_rows(64, 128), finer[0], (((1,), (1,)), ((), ())), preferred_element_type=jnp.float32
    ).astype(jnp.bfloat16)
    fifth_ref[...] = fifth
    finer = fifth
    ready_ref[0] = jnp.zeros((32, 128), jnp.bfloat16)
    for level in (6, 7, 8):
        finer = mm(halving_rows(32, finer.shape[0]), finer).astype(jnp.bfloat16)
        ready_ref[level - 5] = finer
    for there in range(16):
        far_ref[there] = ready_ref[needed_level(plane, there) - 5]


def needed_level(plane, there):
    level = jnp.int32(8)
    for at in (7, 6, 5):
        near = jnp.abs((plane >> (at - 5)) - (there >> (at - 5))) <= 1
        level = jnp.where(near, jnp.int32(at), level)
    return level


class Task:
    def __init__(self, level, query, keys, values, bias=None):
        self.level, self.query, self.keys, self.values = level, query, keys, values
        self.bias = bias or [None] * len(keys)
        self.rows = 128 * len(keys)


def biased(scores, add):
    return scores if add is None else scores + add


def softmax_parts(parts):
    top = parts[0].max(axis=0, keepdims=True)
    for part in parts[1:]:
        top = jnp.maximum(top, part.max(axis=0, keepdims=True))
    top = top * SCALE
    weights, total = [], None
    for part in parts:
        grown = jnp.exp2(part * SCALE - top)
        added = grown.sum(axis=0, keepdims=True)
        total = added if total is None else total + added
        weights.append(grown.astype(jnp.bfloat16))
    return top, total, weights


def attend_all(tasks, score_ref, weight_ref):
    lower = iota((64, 128), 1) < 64
    none = jnp.zeros((64, 128), jnp.bfloat16)
    for n, task in enumerate(tasks):
        score_ref[n, : task.rows] = mm(jnp.concatenate(task.keys, axis=0), task.query)
    tops = []
    for n, task in enumerate(tasks):
        if task.level == 0:
            parts = [biased(score_ref[n, 128 * i : 128 * i + 128], add) for i, add in enumerate(task.bias)]
            top, total, weights = softmax_parts(parts)
            for i, weight in enumerate(weights):
                weight_ref[n, 128 * i : 128 * i + 128] = weight
        else:
            first, second, third, fourth = (
                biased(score_ref[n, 64 * i : 64 * i + 64], task.bias[i // 2]) for i in range(4)
            )
            top, total, weights = softmax_parts([first, jnp.where(lower, third, second), fourth])
            weight_ref[n, 0:64] = weights[0]
            weight_ref[n, 64:128] = jnp.where(lower, none, weights[1])
            weight_ref[n, 128:192] = jnp.where(lower, weights[1], none)
            weight_ref[n, 192:256] = weights[2]
        tops.append((top, total))
    states = []
    for n, task in enumerate(tasks):
        numer = mm(jnp.concatenate(task.values, axis=1), weight_ref[n, : task.rows])
        times = 2.0**task.level
        top, total = tops[n]
        states.append((numer * times, top, total * times) if task.level else (numer, top, total))
    return states


def put(ref, place, state):
    numer, top, total = state
    ref[place, :64] = numer
    ref[place, 64:65] = top
    ref[place, 65:66] = total


def get(ref, place):
    return ref[place, :64], ref[place, 64:65], ref[place, 65:66]


def merge(one, two):
    top = jnp.maximum(one[1], two[1])
    scale_one = jnp.exp2(one[1] - top)
    scale_two = jnp.exp2(two[1] - top)
    return one[0] * scale_one + two[0] * scale_two, top, one[2] * scale_one + two[2] * scale_two


def lanes_from(state, picks):
    wide = jnp.concatenate([picks] * 8, axis=0)
    both = jnp.concatenate([state[1], state[2], jnp.zeros((6, 128), jnp.float32)], axis=0)
    both = jnp.take_along_axis(both, picks, axis=1)
    return jnp.take_along_axis(state[0], wide, axis=1), both[0:1], both[1:2]


STATE_TILES = TILES + 8 + 4
STATE_AT = {0: 0, 1: 16, 2: 24}


def level_tile(level_zero, coarse, level, i):
    return level_zero.at[i] if level == 0 else coarse.at[OFFSET[level] + i]


def query_tile(level_zero, coarse, level, i):
    return level_zero[i, 128:] if level == 0 else coarse[OFFSET[level] + i]


def interior_kernel(
    x_ref, tiles_ref, fifth_ref, state_ref, coarse_q_ref, packed_ref, inside_ref, outside_ref, score_ref, weight_ref
):
    first_core = (lax.axis_index("seqhi") & 1) == 0
    for level in range(5):
        first = level_tile(x_ref, tiles_ref, level, 0)[:128]
        last = level_tile(x_ref, tiles_ref, level, COUNT[level] - 1)[:128]
        inside_ref[level] = jnp.where(first_core, last, first)
        sent = jnp.where(first_core, first, last)
        outside_ref[2 * level] = sent[:64]
        outside_ref[2 * level + 1] = sent[64:]
    outside_ref[10] = fifth_ref[...]
    halve = halving()
    finer = [x_ref[i, 128:] for i in range(TILES)]
    for level in range(1, 5):
        finer = coarser_tiles(finer, halve)
        for i, tile in enumerate(finer):
            coarse_q_ref[OFFSET[level] + i] = tile
    tile, packed = finer[0], None
    lanes = iota((64, 128), 1)
    for level in range(5, 9):
        tile = mm(tile, halve[:128]).astype(jnp.bfloat16)
        wide = tile.astype(jnp.float32)
        if level == 5:
            packed = wide
        else:
            packed = jnp.where(lanes >= PACKED[level], pltpu.roll(wide, PACKED[level], 1), packed)
    packed_ref[...] = packed.astype(jnp.bfloat16)

    tasks, places = [], []
    for level in range(3):
        turned = [level_tile(x_ref, tiles_ref, level, n)[:64].T for n in range(COUNT[level])]
        for i in range(1, COUNT[level] - 1):
            at = (i - 1, i, i + 1) if level == 0 else (i - 1, i + 1)
            values = [level_tile(x_ref, tiles_ref, level, n)[64:128] for n in at]
            tasks.append(Task(level, query_tile(x_ref, coarse_q_ref, level, i), [turned[n] for n in at], values))
            places.append(STATE_AT[level] + i)
    for place, state in zip(places, attend_all(tasks, score_ref, weight_ref)):
        put(state_ref, place, state)


def edges_kernel(
    coarse_q_ref, x_ref, tiles_ref, inside_ref, outside_ref, inner_ref, state_ref, score_ref, weight_ref
):
    place = lax.axis_index("seqhi")
    last_place = lax.axis_size("seqhi") - 1
    first_core = (place & 1) == 0
    no_before = jnp.where(place == 0, jnp.float32(NEVER), jnp.float32(0.0))
    no_after = jnp.where(place == last_place, jnp.float32(NEVER), jnp.float32(0.0))
    lanes = iota((8, 128), 1)

    def side(level, i):
        if 0 <= i < COUNT[level]:
            ref = level_tile(x_ref, tiles_ref, level, i)
            return ref[:64].T, ref[64:128], None
        came_inside = first_core if i >= 0 else jnp.logical_not(first_core)
        key = jnp.where(came_inside, inside_ref[level, :64], outside_ref[2 * level])
        value = jnp.where(came_inside, inside_ref[level, 64:], outside_ref[2 * level + 1])
        return key.T, value, no_before if i < 0 else no_after

    tasks, places = [], []
    for level in (4, 3, 2, 1, 0):
        for i in range(COUNT[level]):
            if level < 3 and 0 < i < COUNT[level] - 1:
                continue
            at = (i - 1, i, i + 1) if level == 0 else (i - 1, i + 1)
            keys, values, bias = zip(*(side(level, n) for n in at))
            tasks.append(Task(level, query_tile(x_ref, coarse_q_ref, level, i), keys, values, bias))
            places.append((level, i))
    done = dict(zip(places, attend_all(tasks, score_ref, weight_ref)))
    coarser = None
    for level in (4, 3, 2, 1, 0):
        merged = []
        for i in range(COUNT[level]):
            state = done[level, i] if (level, i) in done else get(inner_ref, STATE_AT[level] + i)
            if coarser is not None:
                state = merge(state, lanes_from(coarser[i // 2], 64 * (i % 2) + lanes // 2))
            merged.append(state)
        coarser = merged
    for i in range(TILES):
        put(state_ref, i, coarser[i])


def lane_levels():
    lane = iota((32, 128), 1)
    return jnp.where(lane < 64, 5, jnp.where(lane < 96, 6, jnp.where(lane < 112, 7, 8)))


def far_state(plane, query, chunks_ref, near, bias_ref, score_ref):
    slot = iota((32, 128), 0)
    lane_level = lane_levels()
    bias_ref[0] = jnp.full((32, 128), NEVER, jnp.float32)
    for level in (6, 7, 8):
        held = (lane_level == level) & (slot < (64 >> (level - 5)))
        bias_ref[level - 5] = jnp.where(held, 0.0, NEVER)
    first_lanes = jnp.where(iota((1, 128), 1) < 64, 0.0, NEVER)
    tall = jnp.concatenate([query, jnp.zeros((64, 128), jnp.bfloat16)], axis=0)
    rows = jnp.concatenate([chunks_ref[...]] + [tile for tile, _ in near], axis=0)
    count = rows.shape[0]
    score_ref[:count] = mm(rows, tall)
    top = None
    for n in range(16 + 2 * len(near)):
        if n < 16:
            bias = bias_ref[needed_level(plane, n) - 5]
        else:
            bias = first_lanes + jnp.where(near[(n - 16) // 2][1], 0.0, NEVER)
        part = score_ref[32 * n : 32 * n + 32] + bias
        score_ref[32 * n : 32 * n + 32] = part
        high = part.max(axis=0, keepdims=True)
        top = high if top is None else jnp.maximum(top, high)
    top = top * SCALE
    grown = jnp.exp2(score_ref[:count] * SCALE - top)
    total = grown.sum(axis=0, keepdims=True)
    both = lax.dot_general(
        rows, grown.astype(jnp.bfloat16), (((0,), (0,)), ((), ())), preferred_element_type=jnp.float32
    )
    return both[64:], top, total


def own_kernel(packed_ref, chunks_ref, beyond_ref, state_ref, bias_ref, score_ref):
    place = lax.axis_index("seqhi")
    toward = jnp.where((place & 1) == 0, place - 2, place + 2)
    near = [(beyond_ref[...], (toward >= 0) & (toward < lax.axis_size("seqhi")))]
    put(state_ref, 0, far_state(place >> 1, packed_ref[...], chunks_ref, near, bias_ref, score_ref))


def final_kernel(packed_ref, other_ref, own_ref, local_ref, out_ref, bias_ref, score_ref):
    place = lax.axis_index("seqhi")
    toward = jnp.where((place & 1) == 0, place + 2, place - 2)
    here = (toward >= 0) & (toward < lax.axis_size("seqhi"))
    near = [(other_ref[512:576], here), (other_ref[576:], here)]
    state = far_state(place >> 1, packed_ref[...], other_ref.at[:512], near, bias_ref, score_ref)
    numer, top, total = merge(state, get(own_ref, 0))
    row = lane_levels()[:1]
    times = jnp.where(row == 5, 32.0, jnp.where(row == 6, 64.0, jnp.where(row == 7, 128.0, 256.0)))
    packed = (numer * times, top, total * times)
    lanes = iota((8, 128), 1)
    state = packed
    for level in (6, 7, 8):
        picks = jnp.minimum(PACKED[level] + lanes // (1 << (level - 5)), 127)
        state = merge(state, lanes_from(packed, picks))
    for i in range(TILES):
        spread = lanes_from(state, 4 * i + lanes // 32)
        numer, _, total = merge(get(local_ref, i), spread)
        out_ref[i] = (numer / total).astype(jnp.bfloat16)


def call(kernel, out_shape, in_specs, flops, moved, exps=0, scratch=(), limit=24, out_specs=VMEM):
    if isinstance(out_shape, tuple):
        out_specs = (out_specs,) * len(out_shape)
    return pl.pallas_call(
        kernel,
        out_shape=out_shape,
        in_specs=in_specs,
        out_specs=out_specs,
        scratch_shapes=scratch,
        compiler_params=pltpu.CompilerParams(vmem_limit_bytes=limit << 20),
        cost_estimate=pl.CostEstimate(flops=flops, bytes_accessed=moved, transcendentals=exps),
    )


def split(key_rows, value_rows, queries):
    hbm = pl.BlockSpec(memory_space=pltpu.HBM)
    scratch = [
        pltpu.VMEM((3, 128, HEADS * HEAD), jnp.bfloat16),
        pltpu.VMEM((HEADS, 192, 128), jnp.bfloat16),
        pltpu.SemaphoreType.DMA((3,)),
        pltpu.SemaphoreType.DMA((3,)),
    ]
    out = jax.ShapeDtypeStruct((HEADS, 192, 128), jnp.bfloat16)
    return call(split_kernel, out, [hbm] * 3, 1 << 22, 3 << 19, 0, scratch, 62, hbm)(key_rows, value_rows, queries)


def body(queries, key_rows, value_rows):
    bf16, f32 = jnp.bfloat16, jnp.float32
    outer = lax.axis_size("seqhi")
    shape = jax.ShapeDtypeStruct

    tokens = lax.all_to_all(split(key_rows, value_rows, queries), "seqlo", 0, 0)

    far, fifth, tiles = call(
        coarse_kernel,
        (shape((16, 32, 128), bf16), shape((64, 128), bf16), shape((15, 128, 128), bf16)),
        [VMEM],
        1 << 27,
        2 << 20,
        scratch=[pltpu.VMEM((4, 32, 128), bf16)],
    )(tokens)

    planes = [[2 * z + core for z in range(outer // 2)] for core in range(2)]
    own = lax.all_to_all(far, "seqhi", 0, 0, axis_index_groups=planes)
    inner, coarse_q, packed, inside, outside = call(
        interior_kernel,
        (
            shape((STATE_TILES, ROWS, 128), f32),
            shape((15, 64, 128), bf16),
            shape((64, 128), bf16),
            shape((5, 128, 128), bf16),
            shape((11, 64, 128), bf16),
        ),
        [VMEM] * 3,
        1 << 20,
        1 << 16,
        1 << 10,
        [pltpu.VMEM((22, 384, 128), f32), pltpu.VMEM((22, 384, 128), bf16)],
    )(tokens, tiles, fifth)
    beside = [pair for i in range(1, outer - 1, 2) for pair in ((i, i + 1), (i + 1, i))]
    outside = lax.ppermute(outside, "seqhi", beside)
    cores = [(i, i ^ 1) for i in range(outer)]
    inside = lax.ppermute(inside, "seqhi", cores)
    apart = [(i, i + 2) for i in range(0, outer - 2, 2)] + [(i, i - 2) for i in range(3, outer, 2)]
    fifth, inner = lax.optimization_barrier((fifth, inner))
    beyond = lax.ppermute(fifth, "seqhi", apart)
    local = call(
        edges_kernel,
        shape((TILES, ROWS, 128), f32),
        [VMEM] * 6,
        1 << 20,
        1 << 16,
        1 << 10,
        [pltpu.VMEM((9, 384, 128), f32), pltpu.VMEM((9, 384, 128), bf16)],
    )(coarse_q, tokens, tiles, inside, outside, inner)

    own, local = lax.optimization_barrier((own, local))
    own = own.reshape(512, 128)
    other = lax.ppermute(jnp.concatenate([own, outside[10], beyond], axis=0), "seqhi", cores)
    scratch = [pltpu.VMEM((4, 32, 128), f32), pltpu.VMEM((640, 128), f32)]
    own_state = call(
        own_kernel, shape((1, ROWS, 128), f32), [VMEM] * 3, 1 << 30, 1 << 20, 1 << 17, scratch
    )(packed, own, beyond)
    out = call(
        final_kernel, shape((TILES, HEAD, 128), bf16), [VMEM] * 4, 1 << 30, 2 << 20, 1 << 17, scratch
    )(packed, other, own_state, local)

    heads = lax.all_to_all(out, "seqlo", 0, 0)
    return call(join_kernel, shape((128, HEADS * HEAD), bf16), [VMEM], 1 << 22, 1 << 19)(heads)


def solution(mesh):
    placed = P(("seqhi", "seqlo"), None)
    return jax.shard_map(body, mesh=mesh, in_specs=(placed,) * 3, out_specs=placed, check_vma=False)
```

```python
import math

import jax
import jax.numpy as jnp
from jax import lax
from jax.experimental import pallas as pl
from jax.experimental.pallas import tpu as pltpu
from jax.sharding import PartitionSpec as P

HEADS = 16
HEAD = 64
BLOCK = 128
NEVER = -1e30
SCALE = math.log2(math.e) / math.sqrt(HEAD)
TILES = 16
OFFSET = {1: 0, 2: 8, 3: 12, 4: 14}
COUNT = {0: 16, 1: 8, 2: 4, 3: 2, 4: 1}
ROWS = 72
PACKED = {5: 0, 6: 64, 7: 96, 8: 112}

VMEM = pl.BlockSpec(memory_space=pltpu.VMEM)


def iota(shape, dim):
    return lax.broadcasted_iota(jnp.int32, shape, dim)


def mm(a, b):
    return jnp.dot(a, b, preferred_element_type=jnp.float32)


def split_kernel(k_ref, v_ref, q_ref, out_ref, held, turned, in_sems, out_sems):
    copies = [pltpu.make_async_copy(ref, held.at[n], in_sems.at[n]) for n, ref in enumerate((k_ref, v_ref, q_ref))]
    for copy in copies:
        copy.start()
    sent = []
    for n, copy in enumerate(copies):
        copy.wait()
        rows = pl.ds(64 * n, 64)
        for pair in range(HEADS // 2):
            both = held[n, :, 128 * pair : 128 * pair + 128].T
            turned[2 * pair, rows, :] = both[:64]
            turned[2 * pair + 1, rows, :] = both[64:]
        out = pltpu.make_async_copy(turned.at[:, rows], out_ref.at[:, rows], out_sems.at[n])
        out.start()
        sent.append(out)
    for out in sent:
        out.wait()


def join_kernel(in_ref, out_ref):
    for pair in range(HEADS // 2):
        both = jnp.concatenate([in_ref[2 * pair], in_ref[2 * pair + 1]], axis=0)
        out_ref[:, 128 * pair : 128 * pair + 128] = both.T


def halving():
    wanted = iota((256, 128), 0) // 2 == iota((256, 128), 1)
    return jnp.where(wanted, 0.5, 0.0).astype(jnp.bfloat16)


def halving_rows(rows, columns):
    return jnp.where(iota((rows, columns), 1) // 2 == iota((rows, columns), 0), 0.5, 0.0).astype(jnp.bfloat16)


def coarser_tiles(finer, halve):
    pairs = [jnp.concatenate([finer[i], finer[i + 1]], axis=1) for i in range(0, len(finer), 2)]
    return [mm(pair, halve).astype(jnp.bfloat16) for pair in pairs]


def coarse_kernel(x_ref, far_ref, fifth_ref, tiles_ref, ready_ref):
    place = lax.axis_index("seqhi")
    plane = place >> 1
    halve = halving()
    finer = [x_ref[i, :128] for i in range(TILES)]
    for level in range(1, 5):
        finer = coarser_tiles(finer, halve)
        for i, tile in enumerate(finer):
            tiles_ref[OFFSET[level] + i] = tile
    fifth = lax.dot_general(
        halving_rows(64, 128), finer[0], (((1,), (1,)), ((), ())), preferred_element_type=jnp.float32
    ).astype(jnp.bfloat16)
    fifth_ref[...] = fifth
    finer = fifth
    ready_ref[0] = jnp.zeros((32, 128), jnp.bfloat16)
    for level in (6, 7, 8):
        finer = mm(halving_rows(32, finer.shape[0]), finer).astype(jnp.bfloat16)
        ready_ref[level - 5] = finer
    for there in range(16):
        far_ref[there] = ready_ref[needed_level(plane, there) - 5]


def needed_level(plane, there):
    level = jnp.int32(8)
    for at in (7, 6, 5):
        near = jnp.abs((plane >> (at - 5)) - (there >> (at - 5))) <= 1
        level = jnp.where(near, jnp.int32(at), level)
    return level


class Task:
    def __init__(self, level, query, keys, values, bias=None):
        self.level, self.query, self.keys, self.values = level, query, keys, values
        self.bias = bias or [None] * len(keys)
        self.rows = 128 * len(keys)


def biased(scores, add):
    return scores if add is None else scores + add


def softmax_parts(parts):
    top = parts[0].max(axis=0, keepdims=True)
    for part in parts[1:]:
        top = jnp.maximum(top, part.max(axis=0, keepdims=True))
    top = top * SCALE
    weights, total = [], None
    for part in parts:
        grown = jnp.exp2(part * SCALE - top)
        added = grown.sum(axis=0, keepdims=True)
        total = added if total is None else total + added
        weights.append(grown.astype(jnp.bfloat16))
    return top, total, weights


def attend_all(tasks, score_ref, weight_ref):
    lower = iota((64, 128), 1) < 64
    none = jnp.zeros((64, 128), jnp.bfloat16)
    for n, task in enumerate(tasks):
        score_ref[n, : task.rows] = mm(jnp.concatenate(task.keys, axis=0), task.query)
    tops = []
    for n, task in enumerate(tasks):
        if task.level == 0:
            parts = [biased(score_ref[n, 128 * i : 128 * i + 128], add) for i, add in enumerate(task.bias)]
            top, total, weights = softmax_parts(parts)
            for i, weight in enumerate(weights):
                weight_ref[n, 128 * i : 128 * i + 128] = weight
        else:
            first, second, third, fourth = (
                biased(score_ref[n, 64 * i : 64 * i + 64], task.bias[i // 2]) for i in range(4)
            )
            top, total, weights = softmax_parts([first, jnp.where(lower, third, second), fourth])
            weight_ref[n, 0:64] = weights[0]
            weight_ref[n, 64:128] = jnp.where(lower, none, weights[1])
            weight_ref[n, 128:192] = jnp.where(lower, weights[1], none)
            weight_ref[n, 192:256] = weights[2]
        tops.append((top, total))
    states = []
    for n, task in enumerate(tasks):
        numer = mm(jnp.concatenate(task.values, axis=1), weight_ref[n, : task.rows])
        times = 2.0**task.level
        top, total = tops[n]
        states.append((numer * times, top, total * times) if task.level else (numer, top, total))
    return states


def put(ref, place, state):
    numer, top, total = state
    ref[place, :64] = numer
    ref[place, 64:65] = top
    ref[place, 65:66] = total


def get(ref, place):
    return ref[place, :64], ref[place, 64:65], ref[place, 65:66]


def merge(one, two):
    top = jnp.maximum(one[1], two[1])
    scale_one = jnp.exp2(one[1] - top)
    scale_two = jnp.exp2(two[1] - top)
    return one[0] * scale_one + two[0] * scale_two, top, one[2] * scale_one + two[2] * scale_two


def lanes_from(state, picks):
    wide = jnp.concatenate([picks] * 8, axis=0)
    both = jnp.concatenate([state[1], state[2], jnp.zeros((6, 128), jnp.float32)], axis=0)
    both = jnp.take_along_axis(both, picks, axis=1)
    return jnp.take_along_axis(state[0], wide, axis=1), both[0:1], both[1:2]


STATE_TILES = TILES + 8 + 4
STATE_AT = {0: 0, 1: 16, 2: 24}


def level_tile(level_zero, coarse, level, i):
    return level_zero.at[i] if level == 0 else coarse.at[OFFSET[level] + i]


def query_tile(level_zero, coarse, level, i):
    return level_zero[i, 128:] if level == 0 else coarse[OFFSET[level] + i]


def prepare_kernel(x_ref, tiles_ref, fifth_ref, inside_ref, outside_ref, coarse_q_ref, packed_ref):
    first_core = (lax.axis_index("seqhi") & 1) == 0
    for level in range(5):
        first = level_tile(x_ref, tiles_ref, level, 0)[:128]
        last = level_tile(x_ref, tiles_ref, level, COUNT[level] - 1)[:128]
        inside_ref[level] = jnp.where(first_core, last, first)
        sent = jnp.where(first_core, first, last)
        outside_ref[2 * level] = sent[:64]
        outside_ref[2 * level + 1] = sent[64:]
    outside_ref[10] = fifth_ref[...]
    halve = halving()
    finer = [x_ref[i, 128:] for i in range(TILES)]
    for level in range(1, 5):
        finer = coarser_tiles(finer, halve)
        for i, tile in enumerate(finer):
            coarse_q_ref[OFFSET[level] + i] = tile
    tile, packed = finer[0], None
    lanes = iota((64, 128), 1)
    for level in range(5, 9):
        tile = mm(tile, halve[:128]).astype(jnp.bfloat16)
        wide = tile.astype(jnp.float32)
        if level == 5:
            packed = wide
        else:
            packed = jnp.where(lanes >= PACKED[level], pltpu.roll(wide, PACKED[level], 1), packed)
    packed_ref[...] = packed.astype(jnp.bfloat16)


def interior_kernel(x_ref, tiles_ref, coarse_q_ref, state_ref, score_ref, weight_ref):
    tasks, places = [], []
    for level in range(3):
        turned = [level_tile(x_ref, tiles_ref, level, n)[:64].T for n in range(COUNT[level])]
        for i in range(1, COUNT[level] - 1):
            at = (i - 1, i, i + 1) if level == 0 else (i - 1, i + 1)
            values = [level_tile(x_ref, tiles_ref, level, n)[64:128] for n in at]
            tasks.append(Task(level, query_tile(x_ref, coarse_q_ref, level, i), [turned[n] for n in at], values))
            places.append(STATE_AT[level] + i)
    for place, state in zip(places, attend_all(tasks, score_ref, weight_ref)):
        put(state_ref, place, state)


def edges_kernel(
    coarse_q_ref, x_ref, tiles_ref, inside_ref, outside_ref, inner_ref, state_ref, score_ref, weight_ref
):
    place = lax.axis_index("seqhi")
    last_place = lax.axis_size("seqhi") - 1
    first_core = (place & 1) == 0
    no_before = jnp.where(place == 0, jnp.float32(NEVER), jnp.float32(0.0))
    no_after = jnp.where(place == last_place, jnp.float32(NEVER), jnp.float32(0.0))
    lanes = iota((8, 128), 1)

    def side(level, i):
        if 0 <= i < COUNT[level]:
            ref = level_tile(x_ref, tiles_ref, level, i)
            return ref[:64].T, ref[64:128], None
        came_inside = first_core if i >= 0 else jnp.logical_not(first_core)
        key = jnp.where(came_inside, inside_ref[level, :64], outside_ref[2 * level])
        value = jnp.where(came_inside, inside_ref[level, 64:], outside_ref[2 * level + 1])
        return key.T, value, no_before if i < 0 else no_after

    tasks, places = [], []
    for level in (4, 3, 2, 1, 0):
        for i in range(COUNT[level]):
            if level < 3 and 0 < i < COUNT[level] - 1:
                continue
            at = (i - 1, i, i + 1) if level == 0 else (i - 1, i + 1)
            keys, values, bias = zip(*(side(level, n) for n in at))
            tasks.append(Task(level, query_tile(x_ref, coarse_q_ref, level, i), keys, values, bias))
            places.append((level, i))
    done = dict(zip(places, attend_all(tasks, score_ref, weight_ref)))
    coarser = None
    for level in (4, 3, 2, 1, 0):
        merged = []
        for i in range(COUNT[level]):
            state = done[level, i] if (level, i) in done else get(inner_ref, STATE_AT[level] + i)
            if coarser is not None:
                state = merge(state, lanes_from(coarser[i // 2], 64 * (i % 2) + lanes // 2))
            merged.append(state)
        coarser = merged
    for i in range(TILES):
        put(state_ref, i, coarser[i])


def lane_levels():
    lane = iota((32, 128), 1)
    return jnp.where(lane < 64, 5, jnp.where(lane < 96, 6, jnp.where(lane < 112, 7, 8)))


def far_state(plane, query, chunks_ref, near, bias_ref, score_ref):
    slot = iota((32, 128), 0)
    lane_level = lane_levels()
    bias_ref[0] = jnp.full((32, 128), NEVER, jnp.float32)
    for level in (6, 7, 8):
        held = (lane_level == level) & (slot < (64 >> (level - 5)))
        bias_ref[level - 5] = jnp.where(held, 0.0, NEVER)
    first_lanes = jnp.where(iota((1, 128), 1) < 64, 0.0, NEVER)
    tall = jnp.concatenate([query, jnp.zeros((64, 128), jnp.bfloat16)], axis=0)
    rows = jnp.concatenate([chunks_ref[...]] + [tile for tile, _ in near], axis=0)
    count = rows.shape[0]
    score_ref[:count] = mm(rows, tall)
    top = None
    for n in range(16 + 2 * len(near)):
        if n < 16:
            bias = bias_ref[needed_level(plane, n) - 5]
        else:
            bias = first_lanes + jnp.where(near[(n - 16) // 2][1], 0.0, NEVER)
        part = score_ref[32 * n : 32 * n + 32] + bias
        score_ref[32 * n : 32 * n + 32] = part
        high = part.max(axis=0, keepdims=True)
        top = high if top is None else jnp.maximum(top, high)
    top = top * SCALE
    grown = jnp.exp2(score_ref[:count] * SCALE - top)
    total = grown.sum(axis=0, keepdims=True)
    both = lax.dot_general(
        rows, grown.astype(jnp.bfloat16), (((0,), (0,)), ((), ())), preferred_element_type=jnp.float32
    )
    return both[64:], top, total


def own_kernel(packed_ref, chunks_ref, beyond_ref, state_ref, bias_ref, score_ref):
    place = lax.axis_index("seqhi")
    toward = jnp.where((place & 1) == 0, place - 2, place + 2)
    near = [(beyond_ref[...], (toward >= 0) & (toward < lax.axis_size("seqhi")))]
    put(state_ref, 0, far_state(place >> 1, packed_ref[...], chunks_ref, near, bias_ref, score_ref))


def final_kernel(packed_ref, other_ref, own_ref, local_ref, out_ref, bias_ref, score_ref):
    place = lax.axis_index("seqhi")
    toward = jnp.where((place & 1) == 0, place + 2, place - 2)
    here = (toward >= 0) & (toward < lax.axis_size("seqhi"))
    near = [(other_ref[512:576], here), (other_ref[576:], here)]
    state = far_state(place >> 1, packed_ref[...], other_ref.at[:512], near, bias_ref, score_ref)
    numer, top, total = merge(state, get(own_ref, 0))
    row = lane_levels()[:1]
    times = jnp.where(row == 5, 32.0, jnp.where(row == 6, 64.0, jnp.where(row == 7, 128.0, 256.0)))
    packed = (numer * times, top, total * times)
    lanes = iota((8, 128), 1)
    state = packed
    for level in (6, 7, 8):
        picks = jnp.minimum(PACKED[level] + lanes // (1 << (level - 5)), 127)
        state = merge(state, lanes_from(packed, picks))
    for i in range(TILES):
        spread = lanes_from(state, 4 * i + lanes // 32)
        numer, _, total = merge(get(local_ref, i), spread)
        out_ref[i] = (numer / total).astype(jnp.bfloat16)


def call(kernel, out_shape, in_specs, flops, moved, exps=0, scratch=(), limit=24, out_specs=VMEM):
    if isinstance(out_shape, tuple):
        out_specs = (out_specs,) * len(out_shape)
    return pl.pallas_call(
        kernel,
        out_shape=out_shape,
        in_specs=in_specs,
        out_specs=out_specs,
        scratch_shapes=scratch,
        compiler_params=pltpu.CompilerParams(vmem_limit_bytes=limit << 20),
        cost_estimate=pl.CostEstimate(flops=flops, bytes_accessed=moved, transcendentals=exps),
    )


def split(key_rows, value_rows, queries):
    hbm = pl.BlockSpec(memory_space=pltpu.HBM)
    scratch = [
        pltpu.VMEM((3, 128, HEADS * HEAD), jnp.bfloat16),
        pltpu.VMEM((HEADS, 192, 128), jnp.bfloat16),
        pltpu.SemaphoreType.DMA((3,)),
        pltpu.SemaphoreType.DMA((3,)),
    ]
    out = jax.ShapeDtypeStruct((HEADS, 192, 128), jnp.bfloat16)
    return call(split_kernel, out, [hbm] * 3, 1 << 22, 3 << 19, 0, scratch, 62, hbm)(key_rows, value_rows, queries)


def body(queries, key_rows, value_rows):
    bf16, f32 = jnp.bfloat16, jnp.float32
    outer = lax.axis_size("seqhi")
    shape = jax.ShapeDtypeStruct

    tokens = lax.all_to_all(split(key_rows, value_rows, queries), "seqlo", 0, 0)

    far, fifth, tiles = call(
        coarse_kernel,
        (shape((16, 32, 128), bf16), shape((64, 128), bf16), shape((15, 128, 128), bf16)),
        [VMEM],
        1 << 27,
        2 << 20,
        scratch=[pltpu.VMEM((4, 32, 128), bf16)],
    )(tokens)

    planes = [[2 * z + core for z in range(outer // 2)] for core in range(2)]
    own = lax.all_to_all(far, "seqhi", 0, 0, axis_index_groups=planes)
    inside, outside, coarse_q, packed = call(
        prepare_kernel,
        (
            shape((5, 128, 128), bf16),
            shape((11, 64, 128), bf16),
            shape((15, 64, 128), bf16),
            shape((64, 128), bf16),
        ),
        [VMEM] * 3,
        1 << 20,
        1 << 16,
    )(tokens, tiles, fifth)
    beside = [pair for i in range(1, outer - 1, 2) for pair in ((i, i + 1), (i + 1, i))]
    outside = lax.ppermute(outside, "seqhi", beside)
    cores = [(i, i ^ 1) for i in range(outer)]
    inside = lax.ppermute(inside, "seqhi", cores)
    apart = [(i, i + 2) for i in range(0, outer - 2, 2)] + [(i, i - 2) for i in range(3, outer, 2)]

    inner = call(
        interior_kernel,
        shape((STATE_TILES, ROWS, 128), f32),
        [VMEM] * 3,
        1 << 20,
        1 << 16,
        1 << 10,
        [pltpu.VMEM((22, 384, 128), f32), pltpu.VMEM((22, 384, 128), bf16)],
    )(tokens, tiles, coarse_q)
    beyond = lax.ppermute(fifth, "seqhi", apart)
    local = call(
        edges_kernel,
        shape((TILES, ROWS, 128), f32),
        [VMEM] * 6,
        1 << 20,
        1 << 16,
        1 << 10,
        [pltpu.VMEM((9, 384, 128), f32), pltpu.VMEM((9, 384, 128), bf16)],
    )(coarse_q, tokens, tiles, inside, outside, inner)

    own, local = lax.optimization_barrier((own, local))
    own = own.reshape(512, 128)
    other = lax.ppermute(jnp.concatenate([own, outside[10], beyond], axis=0), "seqhi", cores)
    scratch = [pltpu.VMEM((4, 32, 128), f32), pltpu.VMEM((640, 128), f32)]
    own_state = call(
        own_kernel, shape((1, ROWS, 128), f32), [VMEM] * 3, 1 << 30, 1 << 20, 1 << 17, scratch
    )(packed, own, beyond)
    out = call(
        final_kernel, shape((TILES, HEAD, 128), bf16), [VMEM] * 4, 1 << 30, 2 << 20, 1 << 17, scratch
    )(packed, other, own_state, local)

    heads = lax.all_to_all(out, "seqlo", 0, 0)
    return call(join_kernel, shape((128, HEADS * HEAD), bf16), [VMEM], 1 << 22, 1 << 19)(heads)


def solution(mesh):
    placed = P(("seqhi", "seqlo"), None)
    return jax.shard_map(body, mesh=mesh, in_specs=(placed,) * 3, out_specs=placed, check_vma=False)
```

```python
import math

import jax
import jax.numpy as jnp
from jax import lax
from jax.experimental import pallas as pl
from jax.experimental.pallas import tpu as pltpu
from jax.sharding import PartitionSpec as P

HEADS = 16
HEAD = 64
BLOCK = 128
NEVER = -1e30
SCALE = math.log2(math.e) / math.sqrt(HEAD)
TILES = 16
OFFSET = {1: 0, 2: 8, 3: 12, 4: 14}
COUNT = {0: 16, 1: 8, 2: 4, 3: 2, 4: 1}
ROWS = 72
PACKED = {5: 0, 6: 64, 7: 96, 8: 112}

VMEM = pl.BlockSpec(memory_space=pltpu.VMEM)


def iota(shape, dim):
    return lax.broadcasted_iota(jnp.int32, shape, dim)


def mm(a, b):
    return jnp.dot(a, b, preferred_element_type=jnp.float32)


def split_kernel(k_ref, v_ref, q_ref, out_ref, held, turned, in_sems, out_sems):
    copies = [pltpu.make_async_copy(ref, held.at[n], in_sems.at[n]) for n, ref in enumerate((k_ref, v_ref, q_ref))]
    for copy in copies:
        copy.start()
    sent = []
    for n, copy in enumerate(copies):
        copy.wait()
        rows = pl.ds(64 * n, 64)
        for pair in range(HEADS // 2):
            both = held[n, :, 128 * pair : 128 * pair + 128].T
            turned[2 * pair, rows, :] = both[:64]
            turned[2 * pair + 1, rows, :] = both[64:]
        out = pltpu.make_async_copy(turned.at[:, rows], out_ref.at[:, rows], out_sems.at[n])
        out.start()
        sent.append(out)
    for out in sent:
        out.wait()


def join_kernel(in_ref, out_ref):
    for pair in range(HEADS // 2):
        both = jnp.concatenate([in_ref[2 * pair], in_ref[2 * pair + 1]], axis=0)
        out_ref[:, 128 * pair : 128 * pair + 128] = both.T


def halving():
    wanted = iota((256, 128), 0) // 2 == iota((256, 128), 1)
    return jnp.where(wanted, 0.5, 0.0).astype(jnp.bfloat16)


def halving_rows(rows, columns):
    return jnp.where(iota((rows, columns), 1) // 2 == iota((rows, columns), 0), 0.5, 0.0).astype(jnp.bfloat16)


def coarser_tiles(finer, halve):
    pairs = [jnp.concatenate([finer[i], finer[i + 1]], axis=1) for i in range(0, len(finer), 2)]
    return [mm(pair, halve).astype(jnp.bfloat16) for pair in pairs]


def coarse_kernel(x_ref, far_ref, fifth_ref, tiles_ref, ready_ref):
    place = lax.axis_index("seqhi")
    plane = place >> 1
    halve = halving()
    finer = [x_ref[i, :128] for i in range(TILES)]
    for level in range(1, 5):
        finer = coarser_tiles(finer, halve)
        for i, tile in enumerate(finer):
            tiles_ref[OFFSET[level] + i] = tile
    fifth = lax.dot_general(
        halving_rows(64, 128), finer[0], (((1,), (1,)), ((), ())), preferred_element_type=jnp.float32
    ).astype(jnp.bfloat16)
    fifth_ref[...] = fifth
    finer = fifth
    ready_ref[0] = jnp.zeros((32, 128), jnp.bfloat16)
    for level in (6, 7, 8):
        finer = mm(halving_rows(32, finer.shape[0]), finer).astype(jnp.bfloat16)
        ready_ref[level - 5] = finer
    for there in range(16):
        far_ref[there] = ready_ref[needed_level(plane, there) - 5]


def needed_level(plane, there):
    level = jnp.int32(8)
    for at in (7, 6, 5):
        near = jnp.abs((plane >> (at - 5)) - (there >> (at - 5))) <= 1
        level = jnp.where(near, jnp.int32(at), level)
    return level


class Task:
    def __init__(self, level, query, keys, values, bias=None):
        self.level, self.query, self.keys, self.values = level, query, keys, values
        self.bias = bias or [None] * len(keys)
        self.rows = 128 * len(keys)


def biased(scores, add):
    return scores if add is None else scores + add


def softmax_parts(parts):
    top = parts[0].max(axis=0, keepdims=True)
    for part in parts[1:]:
        top = jnp.maximum(top, part.max(axis=0, keepdims=True))
    top = top * SCALE
    weights, total = [], None
    for part in parts:
        grown = jnp.exp2(part * SCALE - top)
        added = grown.sum(axis=0, keepdims=True)
        total = added if total is None else total + added
        weights.append(grown.astype(jnp.bfloat16))
    return top, total, weights


def attend_all(tasks, score_ref, weight_ref):
    lower = iota((64, 128), 1) < 64
    none = jnp.zeros((64, 128), jnp.bfloat16)
    for n, task in enumerate(tasks):
        score_ref[n, : task.rows] = mm(jnp.concatenate(task.keys, axis=0), task.query)
    tops = []
    for n, task in enumerate(tasks):
        if task.level == 0:
            parts = [biased(score_ref[n, 128 * i : 128 * i + 128], add) for i, add in enumerate(task.bias)]
            top, total, weights = softmax_parts(parts)
            for i, weight in enumerate(weights):
                weight_ref[n, 128 * i : 128 * i + 128] = weight
        else:
            first, second, third, fourth = (
                biased(score_ref[n, 64 * i : 64 * i + 64], task.bias[i // 2]) for i in range(4)
            )
            top, total, weights = softmax_parts([first, jnp.where(lower, third, second), fourth])
            weight_ref[n, 0:64] = weights[0]
            weight_ref[n, 64:128] = jnp.where(lower, none, weights[1])
            weight_ref[n, 128:192] = jnp.where(lower, weights[1], none)
            weight_ref[n, 192:256] = weights[2]
        tops.append((top, total))
    states = []
    for n, task in enumerate(tasks):
        numer = mm(jnp.concatenate(task.values, axis=1), weight_ref[n, : task.rows])
        times = 2.0**task.level
        top, total = tops[n]
        states.append((numer * times, top, total * times) if task.level else (numer, top, total))
    return states


def put(ref, place, state):
    numer, top, total = state
    ref[place, :64] = numer
    ref[place, 64:65] = top
    ref[place, 65:66] = total


def get(ref, place):
    return ref[place, :64], ref[place, 64:65], ref[place, 65:66]


def merge(one, two):
    top = jnp.maximum(one[1], two[1])
    scale_one = jnp.exp2(one[1] - top)
    scale_two = jnp.exp2(two[1] - top)
    return one[0] * scale_one + two[0] * scale_two, top, one[2] * scale_one + two[2] * scale_two


def lanes_from(state, picks):
    wide = jnp.concatenate([picks] * 8, axis=0)
    both = jnp.concatenate([state[1], state[2], jnp.zeros((6, 128), jnp.float32)], axis=0)
    both = jnp.take_along_axis(both, picks, axis=1)
    return jnp.take_along_axis(state[0], wide, axis=1), both[0:1], both[1:2]


STATE_TILES = TILES + 8 + 4
STATE_AT = {0: 0, 1: 16, 2: 24}


def level_tile(level_zero, coarse, level, i):
    return level_zero.at[i] if level == 0 else coarse.at[OFFSET[level] + i]


def query_tile(level_zero, coarse, level, i):
    return level_zero[i, 128:] if level == 0 else coarse[OFFSET[level] + i]


def prepare_kernel(x_ref, tiles_ref, fifth_ref, inside_ref, outside_ref, coarse_q_ref, packed_ref):
    first_core = (lax.axis_index("seqhi") & 1) == 0
    for level in range(5):
        first = level_tile(x_ref, tiles_ref, level, 0)[:128]
        last = level_tile(x_ref, tiles_ref, level, COUNT[level] - 1)[:128]
        inside_ref[level] = jnp.where(first_core, last, first)
        sent = jnp.where(first_core, first, last)
        outside_ref[2 * level] = sent[:64]
        outside_ref[2 * level + 1] = sent[64:]
    outside_ref[10] = fifth_ref[...]
    halve = halving()
    finer = [x_ref[i, 128:] for i in range(TILES)]
    for level in range(1, 5):
        finer = coarser_tiles(finer, halve)
        for i, tile in enumerate(finer):
            coarse_q_ref[OFFSET[level] + i] = tile
    tile, packed = finer[0], None
    lanes = iota((64, 128), 1)
    for level in range(5, 9):
        tile = mm(tile, halve[:128]).astype(jnp.bfloat16)
        wide = tile.astype(jnp.float32)
        if level == 5:
            packed = wide
        else:
            packed = jnp.where(lanes >= PACKED[level], pltpu.roll(wide, PACKED[level], 1), packed)
    packed_ref[...] = packed.astype(jnp.bfloat16)


def interior_kernel(x_ref, tiles_ref, coarse_q_ref, state_ref, score_ref, weight_ref):
    tasks, places = [], []
    for level in range(3):
        turned = [level_tile(x_ref, tiles_ref, level, n)[:64].T for n in range(COUNT[level])]
        for i in range(1, COUNT[level] - 1):
            at = (i - 1, i, i + 1) if level == 0 else (i - 1, i + 1)
            values = [level_tile(x_ref, tiles_ref, level, n)[64:128] for n in at]
            tasks.append(Task(level, query_tile(x_ref, coarse_q_ref, level, i), [turned[n] for n in at], values))
            places.append(STATE_AT[level] + i)
    for place, state in zip(places, attend_all(tasks, score_ref, weight_ref)):
        put(state_ref, place, state)


def edges_kernel(
    coarse_q_ref, x_ref, tiles_ref, inside_ref, outside_ref, inner_ref, state_ref, score_ref, weight_ref
):
    place = lax.axis_index("seqhi")
    last_place = lax.axis_size("seqhi") - 1
    first_core = (place & 1) == 0
    no_before = jnp.where(place == 0, jnp.float32(NEVER), jnp.float32(0.0))
    no_after = jnp.where(place == last_place, jnp.float32(NEVER), jnp.float32(0.0))
    lanes = iota((8, 128), 1)

    def side(level, i):
        if 0 <= i < COUNT[level]:
            ref = level_tile(x_ref, tiles_ref, level, i)
            return ref[:64].T, ref[64:128], None
        came_inside = first_core if i >= 0 else jnp.logical_not(first_core)
        key = jnp.where(came_inside, inside_ref[level, :64], outside_ref[2 * level])
        value = jnp.where(came_inside, inside_ref[level, 64:], outside_ref[2 * level + 1])
        return key.T, value, no_before if i < 0 else no_after

    tasks, places = [], []
    for level in (4, 3, 2, 1, 0):
        for i in range(COUNT[level]):
            if level < 3 and 0 < i < COUNT[level] - 1:
                continue
            at = (i - 1, i, i + 1) if level == 0 else (i - 1, i + 1)
            keys, values, bias = zip(*(side(level, n) for n in at))
            tasks.append(Task(level, query_tile(x_ref, coarse_q_ref, level, i), keys, values, bias))
            places.append((level, i))
    done = dict(zip(places, attend_all(tasks, score_ref, weight_ref)))
    coarser = None
    for level in (4, 3, 2, 1, 0):
        merged = []
        for i in range(COUNT[level]):
            state = done[level, i] if (level, i) in done else get(inner_ref, STATE_AT[level] + i)
            if coarser is not None:
                state = merge(state, lanes_from(coarser[i // 2], 64 * (i % 2) + lanes // 2))
            merged.append(state)
        coarser = merged
    for i in range(TILES):
        put(state_ref, i, coarser[i])


def lane_levels():
    lane = iota((32, 128), 1)
    return jnp.where(lane < 64, 5, jnp.where(lane < 96, 6, jnp.where(lane < 112, 7, 8)))


def far_scores(plane, query, rows, near, bias_ref, score_ref):
    slot = iota((32, 128), 0)
    lane_level = lane_levels()
    bias_ref[0] = jnp.full((32, 128), NEVER, jnp.float32)
    for level in (6, 7, 8):
        held = (lane_level == level) & (slot < (64 >> (level - 5)))
        bias_ref[level - 5] = jnp.where(held, 0.0, NEVER)
    first_lanes = jnp.where(iota((1, 128), 1) < 64, 0.0, NEVER)
    tall = jnp.concatenate([query, jnp.zeros((64, 128), jnp.bfloat16)], axis=0)
    scores = mm(rows, tall)
    top = None
    for n in range(16 + 2 * len(near)):
        if n < 16:
            bias = bias_ref[needed_level(plane, n) - 5]
        else:
            bias = first_lanes + jnp.where(near[(n - 16) // 2], 0.0, NEVER)
        part = scores[32 * n : 32 * n + 32] + bias
        score_ref[32 * n : 32 * n + 32] = part
        high = part.max(axis=0, keepdims=True)
        top = high if top is None else jnp.maximum(top, high)
    return top


def far_sums(rows, scores, top):
    grown = jnp.exp2(scores * SCALE - top)
    both = lax.dot_general(
        rows, grown.astype(jnp.bfloat16), (((0,), (0,)), ((), ())), preferred_element_type=jnp.float32
    )
    return both[64:], grown.sum(axis=0, keepdims=True)


def own_kernel(packed_ref, chunks_ref, beyond_ref, score_ref, top_ref, rows_ref, bias_ref):
    place = lax.axis_index("seqhi")
    toward = jnp.where((place & 1) == 0, place - 2, place + 2)
    near = [(toward >= 0) & (toward < lax.axis_size("seqhi"))]
    rows_ref[:512] = chunks_ref[...]
    rows_ref[512:] = beyond_ref[...]
    top = far_scores(place >> 1, packed_ref[...], rows_ref[...], near, bias_ref, score_ref)
    top_ref[...] = jnp.broadcast_to(top, (8, 128))


def final_kernel(
    packed_ref, other_ref, own_score_ref, own_top_ref, own_rows_ref, local_ref, out_ref, bias_ref, score_ref
):
    place = lax.axis_index("seqhi")
    toward = jnp.where((place & 1) == 0, place + 2, place - 2)
    here = (toward >= 0) & (toward < lax.axis_size("seqhi"))
    top = far_scores(place >> 1, packed_ref[...], other_ref[...], [here, here], bias_ref, score_ref)
    top = jnp.maximum(top, own_top_ref[:1]) * SCALE
    own_numer, own_total = far_sums(own_rows_ref[...], own_score_ref[...], top)
    numer, total = far_sums(other_ref[...], score_ref[...], top)
    numer, total = numer + own_numer, total + own_total
    row = lane_levels()[:1]
    times = jnp.where(row == 5, 32.0, jnp.where(row == 6, 64.0, jnp.where(row == 7, 128.0, 256.0)))
    packed = (numer * times, top, total * times)
    lanes = iota((8, 128), 1)
    state = packed
    for level in (6, 7, 8):
        picks = jnp.minimum(PACKED[level] + lanes // (1 << (level - 5)), 127)
        state = merge(state, lanes_from(packed, picks))
    for i in range(TILES):
        spread = lanes_from(state, 4 * i + lanes // 32)
        numer, _, total = merge(get(local_ref, i), spread)
        out_ref[i] = (numer / total).astype(jnp.bfloat16)


def call(kernel, out_shape, in_specs, flops, moved, exps=0, scratch=(), limit=24, out_specs=VMEM):
    if isinstance(out_shape, tuple):
        out_specs = (out_specs,) * len(out_shape)
    return pl.pallas_call(
        kernel,
        out_shape=out_shape,
        in_specs=in_specs,
        out_specs=out_specs,
        scratch_shapes=scratch,
        compiler_params=pltpu.CompilerParams(vmem_limit_bytes=limit << 20),
        cost_estimate=pl.CostEstimate(flops=flops, bytes_accessed=moved, transcendentals=exps),
    )


def split(key_rows, value_rows, queries):
    hbm = pl.BlockSpec(memory_space=pltpu.HBM)
    scratch = [
        pltpu.VMEM((3, 128, HEADS * HEAD), jnp.bfloat16),
        pltpu.VMEM((HEADS, 192, 128), jnp.bfloat16),
        pltpu.SemaphoreType.DMA((3,)),
        pltpu.SemaphoreType.DMA((3,)),
    ]
    out = jax.ShapeDtypeStruct((HEADS, 192, 128), jnp.bfloat16)
    return call(split_kernel, out, [hbm] * 3, 1 << 22, 3 << 19, 0, scratch, 62, hbm)(key_rows, value_rows, queries)


def body(queries, key_rows, value_rows):
    bf16, f32 = jnp.bfloat16, jnp.float32
    outer = lax.axis_size("seqhi")
    shape = jax.ShapeDtypeStruct

    tokens = lax.all_to_all(split(key_rows, value_rows, queries), "seqlo", 0, 0)

    far, fifth, tiles = call(
        coarse_kernel,
        (shape((16, 32, 128), bf16), shape((64, 128), bf16), shape((15, 128, 128), bf16)),
        [VMEM],
        1 << 27,
        2 << 20,
        scratch=[pltpu.VMEM((4, 32, 128), bf16)],
    )(tokens)

    planes = [[2 * z + core for z in range(outer // 2)] for core in range(2)]
    own = lax.all_to_all(far, "seqhi", 0, 0, axis_index_groups=planes)
    inside, outside, coarse_q, packed = call(
        prepare_kernel,
        (
            shape((5, 128, 128), bf16),
            shape((11, 64, 128), bf16),
            shape((15, 64, 128), bf16),
            shape((64, 128), bf16),
        ),
        [VMEM] * 3,
        1 << 20,
        1 << 16,
    )(tokens, tiles, fifth)
    beside = [pair for i in range(1, outer - 1, 2) for pair in ((i, i + 1), (i + 1, i))]
    outside = lax.ppermute(outside, "seqhi", beside)
    cores = [(i, i ^ 1) for i in range(outer)]
    inside = lax.ppermute(inside, "seqhi", cores)
    apart = [(i, i + 2) for i in range(0, outer - 2, 2)] + [(i, i - 2) for i in range(3, outer, 2)]

    inner = call(
        interior_kernel,
        shape((STATE_TILES, ROWS, 128), f32),
        [VMEM] * 3,
        1 << 20,
        1 << 16,
        1 << 10,
        [pltpu.VMEM((22, 384, 128), f32), pltpu.VMEM((22, 384, 128), bf16)],
    )(tokens, tiles, coarse_q)
    beyond = lax.ppermute(fifth, "seqhi", apart)
    local = call(
        edges_kernel,
        shape((TILES, ROWS, 128), f32),
        [VMEM] * 6,
        1 << 20,
        1 << 16,
        1 << 10,
        [pltpu.VMEM((9, 384, 128), f32), pltpu.VMEM((9, 384, 128), bf16)],
    )(coarse_q, tokens, tiles, inside, outside, inner)

    own, local = lax.optimization_barrier((own, local))
    own = own.reshape(512, 128)
    other = lax.ppermute(jnp.concatenate([own, outside[10], beyond], axis=0), "seqhi", cores)
    scratch = [pltpu.VMEM((4, 32, 128), f32), pltpu.VMEM((640, 128), f32)]
    own_far = call(
        own_kernel,
        (shape((576, 128), f32), shape((8, 128), f32), shape((576, 128), bf16)),
        [VMEM] * 3,
        1 << 30,
        1 << 20,
        1 << 17,
        scratch[:1],
    )(packed, own, beyond)
    out = call(
        final_kernel, shape((TILES, HEAD, 128), bf16), [VMEM] * 6, 1 << 30, 2 << 20, 1 << 17, scratch
    )(packed, other, *own_far, local)

    heads = lax.all_to_all(out, "seqlo", 0, 0)
    return call(join_kernel, shape((128, HEADS * HEAD), bf16), [VMEM], 1 << 22, 1 << 19)(heads)


def solution(mesh):
    placed = P(("seqhi", "seqlo"), None)
    return jax.shard_map(body, mesh=mesh, in_specs=(placed,) * 3, out_specs=placed, check_vma=False)
```

```python
import math

import jax
import jax.numpy as jnp
from jax import lax
from jax.experimental import pallas as pl
from jax.experimental.pallas import tpu as pltpu
from jax.sharding import PartitionSpec as P

HEADS = 16
HEAD = 64
BLOCK = 128
NEVER = -1e30
SCALE = math.log2(math.e) / math.sqrt(HEAD)
TILES = 16
OFFSET = {1: 0, 2: 8, 3: 12, 4: 14}
COUNT = {0: 16, 1: 8, 2: 4, 3: 2, 4: 1}
ROWS = 72
PACKED = {5: 0, 6: 64, 7: 96, 8: 112}

VMEM = pl.BlockSpec(memory_space=pltpu.VMEM)


def iota(shape, dim):
    return lax.broadcasted_iota(jnp.int32, shape, dim)


def mm(a, b):
    return jnp.dot(a, b, preferred_element_type=jnp.float32)


def split_kernel(k_ref, v_ref, q_ref, out_ref, held, turned, in_sems, out_sems):
    copies = [pltpu.make_async_copy(ref, held.at[n], in_sems.at[n]) for n, ref in enumerate((k_ref, v_ref, q_ref))]
    for copy in copies:
        copy.start()
    sent = []
    for n, copy in enumerate(copies):
        copy.wait()
        rows = pl.ds(64 * n, 64)
        for pair in range(HEADS // 2):
            both = held[n, :, 128 * pair : 128 * pair + 128].T
            turned[2 * pair, rows, :] = both[:64]
            turned[2 * pair + 1, rows, :] = both[64:]
        out = pltpu.make_async_copy(turned.at[:, rows], out_ref.at[:, rows], out_sems.at[n])
        out.start()
        sent.append(out)
    for out in sent:
        out.wait()


def join_kernel(in_ref, out_ref, held, sems):
    sent = []
    for half in range(2):
        for pair in range(4 * half, 4 * half + 4):
            both = jnp.concatenate([in_ref[2 * pair], in_ref[2 * pair + 1]], axis=0)
            held[:, 128 * pair : 128 * pair + 128] = both.T
        columns = pl.ds(512 * half, 512)
        copy = pltpu.make_async_copy(held.at[:, columns], out_ref.at[:, columns], sems.at[half])
        copy.start()
        sent.append(copy)
    for copy in sent:
        copy.wait()


def halving():
    wanted = iota((256, 128), 0) // 2 == iota((256, 128), 1)
    return jnp.where(wanted, 0.5, 0.0).astype(jnp.bfloat16)


def halving_rows(rows, columns):
    return jnp.where(iota((rows, columns), 1) // 2 == iota((rows, columns), 0), 0.5, 0.0).astype(jnp.bfloat16)


def coarser_tiles(finer, halve):
    pairs = [jnp.concatenate([finer[i], finer[i + 1]], axis=1) for i in range(0, len(finer), 2)]
    return [mm(pair, halve).astype(jnp.bfloat16) for pair in pairs]


def coarse_kernel(x_ref, far_ref, fifth_ref, tiles_ref, ready_ref):
    place = lax.axis_index("seqhi")
    plane = place >> 1
    halve = halving()
    finer = [x_ref[i, :128] for i in range(TILES)]
    for level in range(1, 5):
        finer = coarser_tiles(finer, halve)
        for i, tile in enumerate(finer):
            tiles_ref[OFFSET[level] + i] = tile
    fifth = lax.dot_general(
        halving_rows(64, 128), finer[0], (((1,), (1,)), ((), ())), preferred_element_type=jnp.float32
    ).astype(jnp.bfloat16)
    fifth_ref[...] = fifth
    finer = fifth
    ready_ref[0] = jnp.zeros((32, 128), jnp.bfloat16)
    for level in (6, 7, 8):
        finer = mm(halving_rows(32, finer.shape[0]), finer).astype(jnp.bfloat16)
        ready_ref[level - 5] = finer
    for there in range(16):
        far_ref[there] = ready_ref[needed_level(plane, there) - 5]


def needed_level(plane, there):
    level = jnp.int32(8)
    for at in (7, 6, 5):
        near = jnp.abs((plane >> (at - 5)) - (there >> (at - 5))) <= 1
        level = jnp.where(near, jnp.int32(at), level)
    return level


class Task:
    def __init__(self, level, query, keys, values, bias=None):
        self.level, self.query, self.keys, self.values = level, query, keys, values
        self.bias = bias or [None] * len(keys)
        self.rows = 128 * len(keys)


def biased(scores, add):
    return scores if add is None else scores + add


def softmax_parts(parts):
    top = parts[0].max(axis=0, keepdims=True)
    for part in parts[1:]:
        top = jnp.maximum(top, part.max(axis=0, keepdims=True))
    top = top * SCALE
    weights, total = [], None
    for part in parts:
        grown = jnp.exp2(part * SCALE - top)
        added = grown.sum(axis=0, keepdims=True)
        total = added if total is None else total + added
        weights.append(grown.astype(jnp.bfloat16))
    return top, total, weights


def attend_all(tasks, score_ref, weight_ref):
    lower = iota((64, 128), 1) < 64
    none = jnp.zeros((64, 128), jnp.bfloat16)
    for n, task in enumerate(tasks):
        score_ref[n, : task.rows] = mm(jnp.concatenate(task.keys, axis=0), task.query)
    tops = []
    for n, task in enumerate(tasks):
        if task.level == 0:
            parts = [biased(score_ref[n, 128 * i : 128 * i + 128], add) for i, add in enumerate(task.bias)]
            top, total, weights = softmax_parts(parts)
            for i, weight in enumerate(weights):
                weight_ref[n, 128 * i : 128 * i + 128] = weight
        else:
            first, second, third, fourth = (
                biased(score_ref[n, 64 * i : 64 * i + 64], task.bias[i // 2]) for i in range(4)
            )
            top, total, weights = softmax_parts([first, jnp.where(lower, third, second), fourth])
            weight_ref[n, 0:64] = weights[0]
            weight_ref[n, 64:128] = jnp.where(lower, none, weights[1])
            weight_ref[n, 128:192] = jnp.where(lower, weights[1], none)
            weight_ref[n, 192:256] = weights[2]
        tops.append((top, total))
    states = []
    for n, task in enumerate(tasks):
        numer = mm(jnp.concatenate(task.values, axis=1), weight_ref[n, : task.rows])
        times = 2.0**task.level
        top, total = tops[n]
        states.append((numer * times, top, total * times) if task.level else (numer, top, total))
    return states


def put(ref, place, state):
    numer, top, total = state
    ref[place, :64] = numer
    ref[place, 64:65] = top
    ref[place, 65:66] = total


def get(ref, place):
    return ref[place, :64], ref[place, 64:65], ref[place, 65:66]


def merge(one, two):
    top = jnp.maximum(one[1], two[1])
    scale_one = jnp.exp2(one[1] - top)
    scale_two = jnp.exp2(two[1] - top)
    return one[0] * scale_one + two[0] * scale_two, top, one[2] * scale_one + two[2] * scale_two


def lanes_from(state, picks):
    wide = jnp.concatenate([picks] * 8, axis=0)
    both = jnp.concatenate([state[1], state[2], jnp.zeros((6, 128), jnp.float32)], axis=0)
    both = jnp.take_along_axis(both, picks, axis=1)
    return jnp.take_along_axis(state[0], wide, axis=1), both[0:1], both[1:2]


STATE_TILES = TILES + 8 + 4
STATE_AT = {0: 0, 1: 16, 2: 24}


def level_tile(level_zero, coarse, level, i):
    return level_zero.at[i] if level == 0 else coarse.at[OFFSET[level] + i]


def query_tile(level_zero, coarse, level, i):
    return level_zero[i, 128:] if level == 0 else coarse[OFFSET[level] + i]


def prepare_kernel(x_ref, tiles_ref, fifth_ref, inside_ref, outside_ref, coarse_q_ref, packed_ref):
    first_core = (lax.axis_index("seqhi") & 1) == 0
    for level in range(5):
        first = level_tile(x_ref, tiles_ref, level, 0)[:128]
        last = level_tile(x_ref, tiles_ref, level, COUNT[level] - 1)[:128]
        inside_ref[level] = jnp.where(first_core, last, first)
        sent = jnp.where(first_core, first, last)
        outside_ref[2 * level] = sent[:64]
        outside_ref[2 * level + 1] = sent[64:]
    outside_ref[10] = fifth_ref[...]
    halve = halving()
    finer = [x_ref[i, 128:] for i in range(TILES)]
    for level in range(1, 5):
        finer = coarser_tiles(finer, halve)
        for i, tile in enumerate(finer):
            coarse_q_ref[OFFSET[level] + i] = tile
    tile, packed = finer[0], None
    lanes = iota((64, 128), 1)
    for level in range(5, 9):
        tile = mm(tile, halve[:128]).astype(jnp.bfloat16)
        wide = tile.astype(jnp.float32)
        if level == 5:
            packed = wide
        else:
            packed = jnp.where(lanes >= PACKED[level], pltpu.roll(wide, PACKED[level], 1), packed)
    packed_ref[...] = packed.astype(jnp.bfloat16)


def interior_kernel(x_ref, tiles_ref, coarse_q_ref, state_ref, score_ref, weight_ref):
    tasks, places = [], []
    for level in range(3):
        turned = [level_tile(x_ref, tiles_ref, level, n)[:64].T for n in range(COUNT[level])]
        for i in range(1, COUNT[level] - 1):
            at = (i - 1, i, i + 1) if level == 0 else (i - 1, i + 1)
            values = [level_tile(x_ref, tiles_ref, level, n)[64:128] for n in at]
            tasks.append(Task(level, query_tile(x_ref, coarse_q_ref, level, i), [turned[n] for n in at], values))
            places.append(STATE_AT[level] + i)
    for place, state in zip(places, attend_all(tasks, score_ref, weight_ref)):
        put(state_ref, place, state)


def edges_kernel(
    coarse_q_ref, x_ref, tiles_ref, inside_ref, outside_ref, inner_ref, state_ref, score_ref, weight_ref
):
    place = lax.axis_index("seqhi")
    last_place = lax.axis_size("seqhi") - 1
    first_core = (place & 1) == 0
    no_before = jnp.where(place == 0, jnp.float32(NEVER), jnp.float32(0.0))
    no_after = jnp.where(place == last_place, jnp.float32(NEVER), jnp.float32(0.0))
    lanes = iota((8, 128), 1)

    def side(level, i):
        if 0 <= i < COUNT[level]:
            ref = level_tile(x_ref, tiles_ref, level, i)
            return ref[:64].T, ref[64:128], None
        came_inside = first_core if i >= 0 else jnp.logical_not(first_core)
        key = jnp.where(came_inside, inside_ref[level, :64], outside_ref[2 * level])
        value = jnp.where(came_inside, inside_ref[level, 64:], outside_ref[2 * level + 1])
        return key.T, value, no_before if i < 0 else no_after

    tasks, places = [], []
    for level in (4, 3, 2, 1, 0):
        for i in range(COUNT[level]):
            if level < 3 and 0 < i < COUNT[level] - 1:
                continue
            at = (i - 1, i, i + 1) if level == 0 else (i - 1, i + 1)
            keys, values, bias = zip(*(side(level, n) for n in at))
            tasks.append(Task(level, query_tile(x_ref, coarse_q_ref, level, i), keys, values, bias))
            places.append((level, i))
    done = dict(zip(places, attend_all(tasks, score_ref, weight_ref)))
    coarser = None
    for level in (4, 3, 2, 1, 0):
        merged = []
        for i in range(COUNT[level]):
            state = done[level, i] if (level, i) in done else get(inner_ref, STATE_AT[level] + i)
            if coarser is not None:
                state = merge(state, lanes_from(coarser[i // 2], 64 * (i % 2) + lanes // 2))
            merged.append(state)
        coarser = merged
    for i in range(TILES):
        put(state_ref, i, coarser[i])


def lane_levels():
    lane = iota((32, 128), 1)
    return jnp.where(lane < 64, 5, jnp.where(lane < 96, 6, jnp.where(lane < 112, 7, 8)))


def far_scores(plane, query, rows, near, bias_ref, score_ref):
    slot = iota((32, 128), 0)
    lane_level = lane_levels()
    bias_ref[0] = jnp.full((32, 128), NEVER, jnp.float32)
    for level in (6, 7, 8):
        held = (lane_level == level) & (slot < (64 >> (level - 5)))
        bias_ref[level - 5] = jnp.where(held, 0.0, NEVER)
    first_lanes = jnp.where(iota((1, 128), 1) < 64, 0.0, NEVER)
    tall = jnp.concatenate([query, jnp.zeros((64, 128), jnp.bfloat16)], axis=0)
    scores = mm(rows, tall)
    top = None
    for n in range(16 + 2 * len(near)):
        if n < 16:
            bias = bias_ref[needed_level(plane, n) - 5]
        else:
            bias = first_lanes + jnp.where(near[(n - 16) // 2], 0.0, NEVER)
        part = scores[32 * n : 32 * n + 32] + bias
        score_ref[32 * n : 32 * n + 32] = part
        high = part.max(axis=0, keepdims=True)
        top = high if top is None else jnp.maximum(top, high)
    return top


def far_sums(rows, scores, top):
    grown = jnp.exp2(scores * SCALE - top)
    both = lax.dot_general(
        rows, grown.astype(jnp.bfloat16), (((0,), (0,)), ((), ())), preferred_element_type=jnp.float32
    )
    return both[64:], grown.sum(axis=0, keepdims=True)


def own_kernel(packed_ref, chunks_ref, beyond_ref, score_ref, top_ref, rows_ref, bias_ref):
    place = lax.axis_index("seqhi")
    toward = jnp.where((place & 1) == 0, place - 2, place + 2)
    near = [(toward >= 0) & (toward < lax.axis_size("seqhi"))]
    rows_ref[:512] = chunks_ref[...]
    rows_ref[512:] = beyond_ref[...]
    top = far_scores(place >> 1, packed_ref[...], rows_ref[...], near, bias_ref, score_ref)
    top_ref[...] = jnp.broadcast_to(top, (8, 128))


def final_kernel(
    packed_ref, other_ref, own_score_ref, own_top_ref, own_rows_ref, local_ref, out_ref, bias_ref, score_ref
):
    place = lax.axis_index("seqhi")
    toward = jnp.where((place & 1) == 0, place + 2, place - 2)
    here = (toward >= 0) & (toward < lax.axis_size("seqhi"))
    top = far_scores(place >> 1, packed_ref[...], other_ref[...], [here, here], bias_ref, score_ref)
    top = jnp.maximum(top, own_top_ref[:1]) * SCALE
    own_numer, own_total = far_sums(own_rows_ref[...], own_score_ref[...], top)
    numer, total = far_sums(other_ref[...], score_ref[...], top)
    numer, total = numer + own_numer, total + own_total
    row = lane_levels()[:1]
    times = jnp.where(row == 5, 32.0, jnp.where(row == 6, 64.0, jnp.where(row == 7, 128.0, 256.0)))
    packed = (numer * times, top, total * times)
    lanes = iota((8, 128), 1)
    state = packed
    for level in (6, 7, 8):
        picks = jnp.minimum(PACKED[level] + lanes // (1 << (level - 5)), 127)
        state = merge(state, lanes_from(packed, picks))
    for i in range(TILES):
        spread = lanes_from(state, 4 * i + lanes // 32)
        numer, _, total = merge(get(local_ref, i), spread)
        out_ref[i] = (numer / total).astype(jnp.bfloat16)


def call(kernel, out_shape, in_specs, flops, moved, exps=0, scratch=(), limit=24, out_specs=VMEM):
    if isinstance(out_shape, tuple):
        out_specs = (out_specs,) * len(out_shape)
    return pl.pallas_call(
        kernel,
        out_shape=out_shape,
        in_specs=in_specs,
        out_specs=out_specs,
        scratch_shapes=scratch,
        compiler_params=pltpu.CompilerParams(vmem_limit_bytes=limit << 20),
        cost_estimate=pl.CostEstimate(flops=flops, bytes_accessed=moved, transcendentals=exps),
    )


def split(key_rows, value_rows, queries):
    hbm = pl.BlockSpec(memory_space=pltpu.HBM)
    scratch = [
        pltpu.VMEM((3, 128, HEADS * HEAD), jnp.bfloat16),
        pltpu.VMEM((HEADS, 192, 128), jnp.bfloat16),
        pltpu.SemaphoreType.DMA((3,)),
        pltpu.SemaphoreType.DMA((3,)),
    ]
    out = jax.ShapeDtypeStruct((HEADS, 192, 128), jnp.bfloat16)
    return call(split_kernel, out, [hbm] * 3, 1 << 22, 3 << 19, 0, scratch, 62, hbm)(key_rows, value_rows, queries)


def body(queries, key_rows, value_rows):
    bf16, f32 = jnp.bfloat16, jnp.float32
    outer = lax.axis_size("seqhi")
    shape = jax.ShapeDtypeStruct

    tokens = lax.all_to_all(split(key_rows, value_rows, queries), "seqlo", 0, 0)

    far, fifth, tiles = call(
        coarse_kernel,
        (shape((16, 32, 128), bf16), shape((64, 128), bf16), shape((15, 128, 128), bf16)),
        [VMEM],
        1 << 27,
        2 << 20,
        scratch=[pltpu.VMEM((4, 32, 128), bf16)],
    )(tokens)

    planes = [[2 * z + core for z in range(outer // 2)] for core in range(2)]
    own = lax.all_to_all(far, "seqhi", 0, 0, axis_index_groups=planes)
    inside, outside, coarse_q, packed = call(
        prepare_kernel,
        (
            shape((5, 128, 128), bf16),
            shape((11, 64, 128), bf16),
            shape((15, 64, 128), bf16),
            shape((64, 128), bf16),
        ),
        [VMEM] * 3,
        1 << 20,
        1 << 16,
    )(tokens, tiles, fifth)
    beside = [pair for i in range(1, outer - 1, 2) for pair in ((i, i + 1), (i + 1, i))]
    outside = lax.ppermute(outside, "seqhi", beside)
    cores = [(i, i ^ 1) for i in range(outer)]
    inside = lax.ppermute(inside, "seqhi", cores)
    apart = [(i, i + 2) for i in range(0, outer - 2, 2)] + [(i, i - 2) for i in range(3, outer, 2)]

    inner = call(
        interior_kernel,
        shape((STATE_TILES, ROWS, 128), f32),
        [VMEM] * 3,
        1 << 20,
        1 << 16,
        1 << 10,
        [pltpu.VMEM((22, 384, 128), f32), pltpu.VMEM((22, 384, 128), bf16)],
    )(tokens, tiles, coarse_q)
    beyond = lax.ppermute(fifth, "seqhi", apart)
    local = call(
        edges_kernel,
        shape((TILES, ROWS, 128), f32),
        [VMEM] * 6,
        1 << 20,
        1 << 16,
        1 << 10,
        [pltpu.VMEM((9, 384, 128), f32), pltpu.VMEM((9, 384, 128), bf16)],
    )(coarse_q, tokens, tiles, inside, outside, inner)

    own, local = lax.optimization_barrier((own, local))
    own = own.reshape(512, 128)
    other = lax.ppermute(jnp.concatenate([own, outside[10], beyond], axis=0), "seqhi", cores)
    scratch = [pltpu.VMEM((4, 32, 128), f32), pltpu.VMEM((640, 128), f32)]
    own_far = call(
        own_kernel,
        (shape((576, 128), f32), shape((8, 128), f32), shape((576, 128), bf16)),
        [VMEM] * 3,
        1 << 30,
        1 << 20,
        1 << 17,
        scratch[:1],
    )(packed, own, beyond)
    out = call(
        final_kernel, shape((TILES, HEAD, 128), bf16), [VMEM] * 6, 1 << 30, 2 << 20, 1 << 17, scratch
    )(packed, other, *own_far, local)

    heads = lax.all_to_all(out, "seqlo", 0, 0)
    scratch = [pltpu.VMEM((128, HEADS * HEAD), bf16), pltpu.SemaphoreType.DMA((2,))]
    hbm = pl.BlockSpec(memory_space=pltpu.HBM)
    return call(join_kernel, shape((128, HEADS * HEAD), bf16), [VMEM], 1 << 22, 1 << 19, 0, scratch, 24, hbm)(heads)


def solution(mesh):
    placed = P(("seqhi", "seqlo"), None)
    return jax.shard_map(body, mesh=mesh, in_specs=(placed,) * 3, out_specs=placed, check_vma=False)
```
